32 devices in a mesh: replica: 2 (over y), tensor: 16 (over z, x, core).
Axes of the slice: x: 2, y: 2, z: 4, core: 2. Of those that a mesh axis runs over, the one named last changes fastest.
Arguments:
- attn_out: bfloat16 [2, 768, 2048], P('replica', None, 'tensor'), may hold values from -6 to 6
- proj: bfloat16 [2, 2048, 2048], P('replica', 'tensor'), may hold values from -6 to 6
- momentum: bfloat16 [2, 2048, 2048], P('replica', 'tensor'), may hold values from -6 to 6
- target: bfloat16 [2, 768, 2048], P('replica'), may hold values from -6 to 6
- segment_ids: int32 [2, 768], P('replica'), may hold values from 0 to 95, never falling along the last dimension, each value on 1 to 192 neighbouring positions
- step: int32 [1], replicated, may hold values from 0 to 999
Outputs:
- projected: bfloat16 [2, 768, 2048], P('replica', 'tensor')
- attn_grad: bfloat16 [2, 768, 2048], P('replica', None, 'tensor')
- new_proj: bfloat16 [2, 2048, 2048], P('replica', 'tensor')
- new_moment: bfloat16 [2, 2048, 2048], P('replica', 'tensor')
The draws below stay inside these ranges and needn't reach their ends.
All inputs are finite; a program needn't handle non-finite values.
Results may differ from the reference program's by a relative error of at most 0.0055.
Values may be sent and summed in bfloat16 or wider, within the bound.
A program may use at most 64 MiB of HBM per device.

```python
import math
import jax
import jax.numpy as jnp
import numpy as np
from jax import lax

HD = 128
HEADS_DEV = 1
DW = 2048
TOK = 768
HEADS = 16
SEGS = 96
SEG_MOST = 192
N_REPLICA = 2
N_TENSOR = 16


def block_levels(own_key, dims, shards, low, largest):
    def one(dim, blocks):
        draws = jax.random.uniform(jax.random.fold_in(jax.random.fold_in(own_key, 6), dim), (blocks,), jnp.float32, low / len(shards), largest / len(shards))
        return jnp.repeat(jnp.exp(draws), dims[dim] // blocks).reshape((-1,) + (1,) * (len(dims) - dim - 1))

    factor_of = one(*shards[0])
    for cut in shards[1:]:
        factor_of = factor_of * one(*cut)
    return factor_of


def length_profile(amount, total, bound, slope):
    portions = [(1 << 20) // math.isqrt(rank ** slope) + 1 for rank in range(2, amount + 1)]
    spare, given = total - bound - (amount - 1), [1] * (amount - 1)
    while spare > 0:
        candidates = [i for i in range(amount - 1) if given[i] < bound]
        mass, budget = sum([portions[i] for i in candidates]), spare
        for i in candidates:
            extra = min(bound - given[i], max(1, budget * portions[i] // mass), spare)
            given[i] = given[i] + extra
            spare = spare - extra
    return np.array([bound] + given)


def ragged(stream_key, number_of, total, bound, skew):
    if number_of == 2:
        one = jax.random.randint(stream_key, (), max(1, total - bound), min(bound, total - 1) + 1)
        return jnp.stack([one, total - one])
    tallies = jnp.asarray(length_profile(number_of, total, bound, skew), jnp.int32)
    pairs = (number_of - 1) // 2
    donor, taker = tallies[1:1 + 2 * pairs:2], tallies[2:2 + 2 * pairs:2]
    margin = jnp.minimum(donor - 1, bound - taker)
    passed = jax.random.randint(jax.random.fold_in(stream_key, 1), (pairs,), 0, 1 << 20) % (margin + 1)
    tallies = tallies.at[1:1 + 2 * pairs:2].set(donor - passed).at[2:2 + 2 * pairs:2].set(taker + passed)
    return tallies[jax.random.permutation(jax.random.fold_in(stream_key, 2), number_of)]


def gaussian(stream_key, dims, deviation, bound, split=(), dtype=jnp.bfloat16):
    entries = jax.random.normal(stream_key, dims, jnp.float32) * deviation
    if len(split) > 0:
        entries = block_levels(stream_key, dims, split, -0.22, 0.18) * entries
    return jnp.clip(entries, min=-bound, max=bound).astype(dtype)


def setup_inputs(seed: int = 0) -> dict:
    key_list = jax.random.split(jax.random.key(seed), 7)
    return {
        "attn_out": gaussian(key_list[0], (N_REPLICA, TOK, HEADS * HD), 1.0, 6.0, ((0, 2), (2, 16))),
        "proj": gaussian(key_list[1], (N_REPLICA, HEADS * HD, DW), 1.0, 6.0, ((0, 2), (1, 16))),
        "momentum": gaussian(key_list[2], (N_REPLICA, HEADS * HD, DW), 1.0, 6.0, ((0, 2), (1, 16))),
        "target": gaussian(key_list[3], (N_REPLICA, TOK, DW), 1.0, 6.0, ((0, 2),)),
        "segment_ids": jax.vmap(lambda own: jnp.searchsorted(jnp.cumsum(ragged(own, SEGS, TOK, SEG_MOST, 2)), jnp.arange(TOK), side="right"))(jax.random.split(key_list[4], N_REPLICA)).reshape((N_REPLICA, TOK)).astype(jnp.int32),
        "step": jax.random.randint(key_list[5], (1,), 0, 1000).astype(jnp.int32),
    }


BETA_MOM = 0.9
STEP_RATE = 0.1


def replica_step(inputs):
    heads_in, weight, moment_in, target_rows, seg_rows = inputs
    head_rows = HEADS_DEV * HD
    scaling = (HEADS * HD) ** -0.5
    blocks_in = heads_in.reshape(TOK, N_TENSOR, head_rows).transpose(1, 0, 2).astype(jnp.float32)
    blocks_w = weight.reshape(N_TENSOR, head_rows, DW).astype(jnp.float32)
    partial_terms = jnp.einsum("ntr,nrd->ntd", blocks_in, blocks_w, precision=lax.Precision.HIGHEST) * scaling
    summed = jnp.sum(partial_terms, axis=0)
    same_doc = (seg_rows[:, None] == seg_rows[None, :]).astype(jnp.float32)
    doc_sizes = jnp.sum(same_doc, axis=1)
    weights = TOK / (SEGS * doc_sizes)
    out_grad = ((summed - target_rows.astype(jnp.float32)) * weights[:, None]).astype(jnp.bfloat16)
    gradient = jnp.dot(heads_in.T, out_grad, preferred_element_type=jnp.float32) * scaling
    attn_grad = (jnp.dot(out_grad, weight.T, preferred_element_type=jnp.float32) * scaling).astype(jnp.bfloat16)
    moment = (BETA_MOM * moment_in.astype(jnp.float32) + gradient).astype(jnp.bfloat16)
    updated = (weight.astype(jnp.float32) - STEP_RATE * moment.astype(jnp.float32)).astype(jnp.bfloat16)
    return summed.astype(jnp.bfloat16), attn_grad, updated, moment


def reference(attn_out, proj, momentum, target, segment_ids, step):
    projected, attn_grad, updated, moment = lax.map(replica_step, (attn_out, proj, momentum, target, segment_ids))
    levels = N_REPLICA.bit_length() - 1
    chosen = (step[0] % levels).astype(jnp.int32)
    hop = jnp.left_shift(jnp.int32(1), chosen)
    partner_proj = jnp.roll(updated, hop, axis=0)
    partner_moment = jnp.roll(moment, hop, axis=0)
    new_proj = ((updated.astype(jnp.float32) + partner_proj.astype(jnp.float32)) * 0.5).astype(jnp.bfloat16)
    new_moment = ((moment.astype(jnp.float32) + partner_moment.astype(jnp.float32)) * 0.5).astype(jnp.bfloat16)
    return projected, attn_grad, new_proj, new_moment
```

```python
import functools
from functools import partial

import jax
import jax.numpy as jnp
from jax import lax
from jax.experimental import pallas as pl
from jax.experimental.pallas import tpu as pltpu
from jax.sharding import PartitionSpec as P

SEGS = 96
BETA_MOM = 0.9
STEP_RATE = 0.1
CHUNKS = 8
BF16 = jnp.bfloat16
F32 = jnp.float32
MESH = pl.DeviceIdType.MESH


def radices_of(size):
    found = []
    while size > 4 and size % 2 == 0:
        found.append(2)
        size //= 2
    if size > 1:
        found.append(size)
    return tuple(found)


def kernel(
    radices,
    replicas,
    chunks,
    mixing,
    scaling,
    attn_ref,
    proj_ref,
    mom_ref,
    seg_ref,
    target_ref,
    projected_ref,
    attn_grad_ref,
    out_proj_ref,
    out_mom_ref,
    *scratch,
):
    levels = len(radices)
    sums = scratch[:levels]
    landed = scratch[levels : 2 * levels]
    (
        grads,
        moments,
        partner_moments,
        partner_proj,
        own_target,
        attn_t,
        total,
        rs_send,
        rs_recv,
        ag_send,
        ag_recv,
        y_send,
        y_recv,
        local_sem,
    ) = scratch[2 * levels :]
    tokens, depth = attn_ref.shape
    width = proj_ref.shape[1] // chunks
    rows = own_target.shape[0]
    me = lax.axis_index("tensor")
    rep = lax.axis_index("replica")
    digits, strides, rest, stride = [], [], me, 1
    for radix in radices:
        digits.append(lax.rem(rest, radix))
        strides.append(stride)
        rest = lax.div(rest, radix)
        stride *= radix

    def peer(level, by):
        to = lax.rem(digits[level] + by, radices[level])
        return to, {"tensor": me + (to - digits[level]) * strides[level]}

    other = {"replica": lax.rem(rep + 1, replicas)}

    barrier = pltpu.get_barrier_semaphore()
    greeted = 0
    for level in range(levels):
        for by in range(1, radices[level]):
            pl.semaphore_signal(barrier, inc=1, device_id=peer(level, by)[1], device_id_type=MESH)
            greeted += 1
    if mixing:
        pl.semaphore_signal(barrier, inc=1, device_id=other, device_id_type=MESH)
        greeted += 1
    fetch = pltpu.make_async_copy(target_ref.at[me], own_target, local_sem)
    fetch.start()

    def columns(k):
        return slice(k * width, (k + 1) * width)

    def product(k):
        part = jnp.dot(attn_ref[...], proj_ref[:, columns(k)], preferred_element_type=F32)
        shape = tuple(reversed(radices)) + (rows, width)
        sums[0][k] = part.reshape(shape).astype(BF16)

    product(0)
    attn_t[...] = attn_ref[...].T
    total[...] = jnp.zeros_like(total)
    pl.semaphore_wait(barrier, greeted)

    proj_copy = None
    if mixing:
        proj_copy = pltpu.make_async_remote_copy(
            src_ref=proj_ref,
            dst_ref=partner_proj,
            send_sem=y_send.at[chunks],
            recv_sem=y_recv.at[chunks],
            device_id=other,
            device_id_type=MESH,
        )
        proj_copy.start()

    seg = seg_ref[...].astype(F32)
    shape = (rows, tokens)
    row_at = lax.broadcasted_iota(jnp.int32, shape, 0) + me * rows
    col_at = lax.broadcasted_iota(jnp.int32, shape, 1)
    seg_all = jnp.broadcast_to(seg, shape)
    own_seg = jnp.sum(jnp.where(row_at == col_at, seg_all, 0.0), axis=1, keepdims=True)
    count = jnp.sum(jnp.where(seg_all == own_seg, 1.0, 0.0), axis=1, keepdims=True)
    weights = tokens / (SEGS * count)

    copies = {}

    def rs_start(level, k):
        high = (slice(None),) * (levels - 1 - level)
        for by in range(1, radices[level]):
            to, device = peer(level, by)
            copy = pltpu.make_async_remote_copy(
                src_ref=sums[level].at[(k,) + high + (to,)],
                dst_ref=landed[level].at[k, by - 1],
                send_sem=rs_send.at[level, k, by - 1],
                recv_sem=rs_recv.at[level, k, by - 1],
                device_id=device,
                device_id_type=MESH,
            )
            copy.start()
            copies["rs", level, k, by] = copy

    def ag_start(level, k):
        high = (slice(None),) * (levels - 1 - level)
        place = (k,) + high + tuple(digits[i] for i in range(level, -1, -1))
        for by in range(1, radices[level]):
            copy = pltpu.make_async_remote_copy(
                src_ref=grads.at[place],
                dst_ref=grads.at[place],
                send_sem=ag_send.at[level, k, by - 1],
                recv_sem=ag_recv.at[level, k, by - 1],
                device_id=peer(level, by)[1],
                device_id_type=MESH,
            )
            copy.start()
            copies["ag", level, k, by] = copy

    def wait_recv(kind, level, k):
        for by in range(1, radices[level]):
            copies[kind, level, k, by].wait_recv()

    def first(k):
        if k > 0:
            product(k)
        rs_start(0, k)

    def reduce_stage(level, k):
        wait_recv("rs", level, k)
        high = (slice(None),) * (levels - 1 - level)
        value = sums[level][(k,) + high + (digits[level],)].astype(F32)
        for by in range(1, radices[level]):
            value = value + landed[level][k, by - 1].astype(F32)
        if level + 1 < levels:
            sums[level + 1][k] = value.astype(BF16)
            rs_start(level + 1, k)
            return
        if k == 0:
            fetch.wait()
        summed = value * scaling
        projected_ref[:, columns(k)] = summed.astype(BF16)
        grad = (summed - own_target[:, columns(k)].astype(F32)) * weights
        grads[(k,) + tuple(reversed(digits))] = grad.astype(BF16)
        ag_start(levels - 1, k)

    def gather_stage(level, k):
        wait_recv("ag", level, k)
        if level > 0:
            ag_start(level - 1, k)
            return
        block = grads[k]
        if rows % 16:
            block = block.astype(F32).reshape(tokens, width).astype(BF16)
        else:
            block = block.reshape(tokens, width)
        gradient = jnp.dot(attn_t[...], block, preferred_element_type=F32) * scaling
        moment = (BETA_MOM * mom_ref[:, columns(k)].astype(F32) + gradient).astype(BF16)
        if mixing:
            moments[k] = moment
            copy = pltpu.make_async_remote_copy(
                src_ref=moments.at[k],
                dst_ref=partner_moments.at[k],
                send_sem=y_send.at[k],
                recv_sem=y_recv.at[k],
                device_id=other,
                device_id_type=MESH,
            )
            copy.start()
            copies["y", k] = copy
        else:
            out_mom_ref[:, columns(k)] = moment
            out_proj_ref[:, columns(k)] = updated_of(proj_ref[:, columns(k)], moment)
        total[...] += lax.dot_general(
            block, proj_ref[:, columns(k)], (((1,), (1,)), ((), ())), preferred_element_type=F32
        )

    def updated_of(weight, moment):
        return (weight.astype(F32) - STEP_RATE * moment.astype(F32)).astype(BF16)

    def mix_stage(k):
        if not mixing:
            return
        if k == 0:
            proj_copy.wait_recv()
        copies["y", k].wait_recv()
        own, theirs = moments[k], partner_moments[k]
        out_mom_ref[:, columns(k)] = ((own.astype(F32) + theirs.astype(F32)) * 0.5).astype(BF16)
        one = updated_of(proj_ref[:, columns(k)], own).astype(F32)
        two = updated_of(partner_proj[:, columns(k)], theirs).astype(F32)
        out_proj_ref[:, columns(k)] = ((one + two) * 0.5).astype(BF16)

    stages = [first]
    stages += [partial(reduce_stage, level) for level in range(levels)]
    stages += [partial(gather_stage, level) for level in range(levels - 1, -1, -1)]
    stages += [mix_stage]
    for step in range(chunks + len(stages) - 1):
        for j, stage in enumerate(stages):
            if 0 <= step - j < chunks:
                stage(step - j)

    attn_grad_ref[...] = (total[...] * scaling).astype(BF16)
    for copy in copies.values():
        copy.wait_send()
    if mixing:
        proj_copy.wait_send()


def fused(attn, proj, mom, seg, target, radices, replicas, mixing):
    tokens, depth = attn.shape
    wide = proj.shape[1]
    size = 1
    for radix in radices:
        size *= radix
    rows = tokens // size
    chunks = CHUNKS
    width = wide // chunks
    levels = len(radices)
    most = max(radices) - 1
    scaling = (depth * size) ** (-0.5)
    sums, landed = [], []
    for level in range(levels):
        high = tuple(reversed(radices[level + 1 :]))
        sums.append(pltpu.VMEM((chunks,) + high + (radices[level], rows, width), BF16))
        landed.append(pltpu.VMEM((chunks, radices[level] - 1) + high + (rows, width), BF16))
    vmem = pl.BlockSpec(memory_space=pltpu.VMEM)
    return pl.pallas_call(
        functools.partial(kernel, radices, replicas, chunks, mixing, scaling),
        out_shape=(
            jax.ShapeDtypeStruct((rows, wide), BF16),
            jax.ShapeDtypeStruct((tokens, depth), BF16),
            jax.ShapeDtypeStruct((depth, wide), BF16),
            jax.ShapeDtypeStruct((depth, wide), BF16),
        ),
        in_specs=[vmem, vmem, vmem, vmem, pl.BlockSpec(memory_space=pl.ANY)],
        out_specs=(vmem, vmem, vmem, vmem),
        scratch_shapes=sums
        + landed
        + [
            pltpu.VMEM((chunks,) + tuple(reversed(radices)) + (rows, width), BF16),
            pltpu.VMEM((chunks, depth, width), BF16),
            pltpu.VMEM((chunks, depth, width), BF16),
            pltpu.VMEM((depth, wide), BF16),
            pltpu.VMEM((rows, wide), BF16),
            pltpu.VMEM((depth, tokens), BF16),
            pltpu.VMEM((tokens, depth), F32),
            pltpu.SemaphoreType.DMA((levels, chunks, most)),
            pltpu.SemaphoreType.DMA((levels, chunks, most)),
            pltpu.SemaphoreType.DMA((levels, chunks, most)),
            pltpu.SemaphoreType.DMA((levels, chunks, most)),
            pltpu.SemaphoreType.DMA((chunks + 1,)),
            pltpu.SemaphoreType.DMA((chunks + 1,)),
            pltpu.SemaphoreType.DMA,
        ],
        cost_estimate=pl.CostEstimate(
            flops=6 * tokens * depth * wide, bytes_accessed=8 * depth * wide, transcendentals=0
        ),
        compiler_params=pltpu.CompilerParams(
            collective_id=0, has_side_effects=True, vmem_limit_bytes=48 * 1024 * 1024
        ),
    )(attn, proj, mom, seg, target)


def passed_along(x, axis, by):
    size = lax.axis_size(axis)
    return lax.ppermute(x, axis, [(i, (i + by) % size) for i in range(size)])


def on_device(attn_out, proj, momentum, target, segment_ids, step):
    tensor_size = lax.axis_size("tensor")
    replicas = lax.axis_size("replica")
    rows_each = target.shape[1] // tensor_size
    bits = replicas.bit_length() - 1
    projected, attn_grad, updated, moment = fused(
        attn_out[0],
        proj[0],
        momentum[0],
        segment_ids,
        target[0].reshape(tensor_size, rows_each, target.shape[2]),
        radices_of(tensor_size),
        replicas,
        replicas == 2,
    )
    if replicas > 2:
        stacked = jnp.stack((updated, moment))
        branches = [
            partial(passed_along, axis="replica", by=1 << bit_pos) for bit_pos in range(bits)
        ]
        partner = lax.switch(step[0] % bits, branches, stacked)
        mixed = ((stacked.astype(F32) + partner.astype(F32)) * 0.5).astype(BF16)
        updated, moment = mixed[0], mixed[1]
    return (projected[None], attn_grad[None], updated[None], moment[None])


def solution(mesh):
    return jax.shard_map(
        on_device,
        mesh=mesh,
        in_specs=(
            P("replica", None, "tensor"),
            P("replica", "tensor", None),
            P("replica", "tensor", None),
            P("replica", None, None),
            P("replica", None),
            P(),
        ),
        out_specs=(
            P("replica", "tensor", None),
            P("replica", None, "tensor"),
            P("replica", "tensor", None),
            P("replica", "tensor", None),
        ),
        check_vma=False,
    )
```

```python
import functools
import itertools
from functools import partial

import jax
import jax.numpy as jnp
from jax import lax
from jax.experimental import pallas as pl
from jax.experimental.pallas import tpu as pltpu
from jax.sharding import PartitionSpec as P

SEGS = 96
BETA_MOM = 0.9
STEP_RATE = 0.1
CHUNKS = 8
AHEAD = 4
VMEM_BYTES = 63 * 1024 * 1024
BF16 = jnp.bfloat16
F32 = jnp.float32
MESH = pl.DeviceIdType.MESH


def radices_of(size):
    found = []
    while size > 2 and size % 2 == 0:
        found.append(2)
        size //= 2
    if size > 1:
        found.append(size)
    return tuple(found)


def kernel(
    radices,
    local,
    replicas,
    chunks,
    mixing,
    scaling,
    attn_hbm,
    proj_hbm,
    mom_hbm,
    seg_ref,
    target_hbm,
    projected_hbm,
    attn_grad_hbm,
    out_proj_hbm,
    out_mom_hbm,
    *scratch,
):
    levels = len(radices)
    outer = levels - local
    sums = scratch[:outer]
    landed = scratch[outer : 2 * outer]
    (
        attn,
        attn_group,
        proj,
        mom,
        target,
        grads,
        moments,
        partner_moments,
        partner_proj,
        attn_t,
        total,
        projected,
        attn_grad,
        out_proj,
        out_mom,
        in_sem,
        proj_sem,
        out_sem,
        a_send,
        a_recv,
        p_send,
        p_recv,
        rs_send,
        rs_recv,
        ag_send,
        ag_recv,
        y_send,
        y_recv,
    ) = scratch[2 * outer :]
    rows, depth = attn.shape[-2:]
    width = proj.shape[-1]
    me = lax.axis_index("tensor")
    rep = lax.axis_index("replica")
    digits, strides, rest, stride = [], [], me, 1
    for radix in radices:
        digits.append(lax.rem(rest, radix))
        strides.append(stride)
        rest = lax.div(rest, radix)
        stride *= radix
    tokens = stride * rows
    mine = tuple(reversed(digits))
    own = tuple(reversed(digits[:local]))
    outer_all = (slice(None),) * outer

    def peer(level, by):
        to = lax.rem(digits[level] + by, radices[level])
        return to, me + (to - digits[level]) * strides[level]

    group = []
    for offsets in itertools.product(*[range(r) for r in reversed(radices[:local])]):
        if any(offsets):
            there, index = [], me
            for level, by in zip(range(local - 1, -1, -1), offsets):
                to, _ = peer(level, by)
                there.append(to)
                index = index + (to - digits[level]) * strides[level]
            group.append((tuple(there), index))

    other = {"replica": lax.rem(rep + 1, replicas)}

    def columns(k):
        return slice(k * width, (k + 1) * width)

    loads = [
        pltpu.make_async_copy(attn_hbm, attn, in_sem.at[0]),
        pltpu.make_async_copy(mom_hbm, mom, in_sem.at[1]),
        pltpu.make_async_copy(target_hbm.at[me], target, in_sem.at[2]),
    ]
    proj_loads = [
        pltpu.make_async_copy(proj_hbm.at[:, columns(k)], proj.at[(k,) + own], proj_sem.at[k])
        for k in range(chunks)
    ]
    loads[0].start()
    for load in proj_loads:
        load.start()
    loads[1].start()
    loads[2].start()

    barrier = pltpu.get_barrier_semaphore()
    greet = [{"tensor": index} for _, index in group]
    for level in range(local, levels):
        greet += [{"tensor": peer(level, by)[1]} for by in range(1, radices[level])]
    if mixing:
        greet.append(other)
    for device in greet:
        pl.semaphore_signal(barrier, inc=1, device_id=device, device_id_type=MESH)
    loads[0].wait()
    pl.semaphore_wait(barrier, len(greet))

    copies = {}

    def send(key, src, dst, send_sem, recv_sem, device):
        copy = pltpu.make_async_remote_copy(
            src_ref=src,
            dst_ref=dst,
            send_sem=send_sem,
            recv_sem=recv_sem,
            device_id=device,
            device_id_type=MESH,
        )
        copy.start()
        copies[key] = copy

    for i, (there, index) in enumerate(group):
        send(
            ("a", i),
            attn.at[outer_all + there],
            attn_group.at[own],
            a_send.at[i],
            a_recv.at[i],
            {"tensor": index},
        )

    def gather(kind, ref, sems, level, k, high):
        place = (k,) + high + tuple(digits[i] for i in range(level, -1, -1))
        for by in range(1, radices[level]):
            send(
                (kind, level, k, by),
                ref.at[place],
                ref.at[place],
                sems[0].at[level, k, by - 1],
                sems[1].at[level, k, by - 1],
                {"tensor": peer(level, by)[1]},
            )

    def share_proj(level, k):
        gather("p", proj, (p_send, p_recv), level, k, (slice(None),) * (local - 1 - level))

    def share_grad(level, k):
        gather("g", grads, (ag_send, ag_recv), level, k, (slice(None),) * (levels - 1 - level))

    def reduce_start(level, k):
        high = (slice(None),) * (levels - 1 - level)
        for by in range(1, radices[level]):
            to, index = peer(level, by)
            send(
                ("r", level, k, by),
                sums[level - local].at[(k,) + high + (to,)],
                landed[level - local].at[k, by - 1],
                rs_send.at[level, k, by - 1],
                rs_recv.at[level, k, by - 1],
                {"tensor": index},
            )

    def wait_recv(kind, level, k):
        for by in range(1, radices[level]):
            copies[kind, level, k, by].wait_recv()

    def first(k):
        proj_loads[k].wait()
        if local > 0:
            share_proj(local - 1, k)

    def proj_stage(level, k):
        wait_recv("p", level, k)
        share_proj(level - 1, k)

    def product(k):
        if local > 0:
            wait_recv("p", 0, k)
        if k == 0:
            for i in range(len(group)):
                copies["a", i].wait_recv()
        part = jnp.zeros((tokens // len_group, width), F32)
        for at in itertools.product(*[range(r) for r in reversed(radices[:local])]):
            left = attn_group[at]
            part = part + jnp.dot(flat(left), proj[(k,) + at], preferred_element_type=F32)
        shape = tuple(reversed(radices[local:])) + (rows, width)
        part = part.reshape(shape)
        if outer > 0:
            sums[0][k] = part.astype(BF16)
            reduce_start(local, k)
        else:
            finish(part, k)

    def flat(block):
        count = 1
        for n in block.shape[:-1]:
            count *= n
        if rows % 16:
            return block.astype(F32).reshape(count, block.shape[-1]).astype(BF16)
        return block.reshape(count, block.shape[-1])

    def reduce_stage(level, k):
        wait_recv("r", level, k)
        high = (slice(None),) * (levels - 1 - level)
        value = sums[level - local][(k,) + high + (digits[level],)].astype(F32)
        for by in range(1, radices[level]):
            value = value + landed[level - local][k, by - 1].astype(F32)
        if level + 1 < levels:
            sums[level + 1 - local][k] = value.astype(BF16)
            reduce_start(level + 1, k)
        else:
            finish(value, k)

    def finish(value, k):
        if k == 0:
            loads[2].wait()
        summed = value * scaling
        grad = (summed - target[:, columns(k)].astype(F32)) * weights
        grads[(k,) + mine] = grad.astype(BF16)
        share_grad(levels - 1, k)
        projected[k] = summed.astype(BF16)
        store(("projected", k), projected.at[k], projected_hbm.at[:, columns(k)], 3 * k)

    stores = []

    def store(key, src, dst, place):
        copy = pltpu.make_async_copy(src, dst, out_sem.at[place])
        copy.start()
        stores.append(copy)

    def gather_stage(level, k):
        wait_recv("g", level, k)
        if level > 0:
            share_grad(level - 1, k)
            return
        if k == 0:
            loads[1].wait()
        block = flat(grads[k])
        weight = proj[(k,) + own]
        gradient = jnp.dot(attn_t[...], block, preferred_element_type=F32) * scaling
        moment = (BETA_MOM * mom[:, columns(k)].astype(F32) + gradient).astype(BF16)
        if mixing:
            moments[k] = moment
            send(
                ("y", k),
                moments.at[k],
                partner_moments.at[k],
                y_send.at[k],
                y_recv.at[k],
                other,
            )
        else:
            put(k, updated_of(weight, moment), moment)
        total[...] += lax.dot_general(
            block, weight, (((1,), (1,)), ((), ())), preferred_element_type=F32
        )

    def put(k, new_proj, new_moment):
        out_proj[k] = new_proj
        out_mom[k] = new_moment
        store(("proj", k), out_proj.at[k], out_proj_hbm.at[:, columns(k)], 3 * k + 1)
        store(("mom", k), out_mom.at[k], out_mom_hbm.at[:, columns(k)], 3 * k + 2)

    def updated_of(weight, moment):
        return (weight.astype(F32) - STEP_RATE * moment.astype(F32)).astype(BF16)

    def mix_stage(k):
        if not mixing:
            return
        if k == 0:
            copies["yp"].wait_recv()
        copies["y", k].wait_recv()
        ours, theirs = moments[k], partner_moments[k]
        one = updated_of(proj[(k,) + own], ours).astype(F32)
        two = updated_of(partner_proj[:, columns(k)], theirs).astype(F32)
        put(
            k,
            ((one + two) * 0.5).astype(BF16),
            ((ours.astype(F32) + theirs.astype(F32)) * 0.5).astype(BF16),
        )

    len_group = len(group) + 1
    stages = [first]
    stages += [partial(proj_stage, level) for level in range(local - 1, 0, -1)]
    stages += [product]
    stages += [partial(reduce_stage, level) for level in range(local, levels)]
    stages += [partial(gather_stage, level) for level in range(levels - 1, -1, -1)]
    stages += [mix_stage]

    ahead = min(AHEAD, chunks)
    for k in range(ahead):
        first(k)
    if mixing:
        send(
            "yp",
            proj_hbm,
            partner_proj,
            y_send.at[chunks],
            y_recv.at[chunks],
            other,
        )
    attn_group[own] = attn[outer_all + own]

    seg = seg_ref[...].astype(F32)
    shape = (rows, tokens)
    row_at = lax.broadcasted_iota(jnp.int32, shape, 0) + me * rows
    col_at = lax.broadcasted_iota(jnp.int32, shape, 1)
    seg_all = jnp.broadcast_to(seg, shape)
    own_seg = jnp.sum(jnp.where(row_at == col_at, seg_all, 0.0), axis=1, keepdims=True)
    count = jnp.sum(jnp.where(seg_all == own_seg, 1.0, 0.0), axis=1, keepdims=True)
    weights = tokens / (SEGS * count)
    attn_t[...] = flat(attn[...]).T
    total[...] = jnp.zeros_like(total)

    for step in range(1, chunks + len(stages) - 1):
        for j, stage in enumerate(stages):
            k = step - j
            if j == 0:
                k = step + ahead - 1
            if 0 <= k < chunks:
                stage(k)

    attn_grad[...] = (total[...] * scaling).astype(BF16)
    store("attn_grad", attn_grad, attn_grad_hbm, 3 * chunks)
    for copy in copies.values():
        copy.wait_send()
    for copy in stores:
        copy.wait()


def fused(attn, proj, mom, seg, target, radices, replicas, mixing):
    size, rows, wide = target.shape
    tokens, depth = size * rows, proj.shape[0]
    chunks = CHUNKS
    width = wide // chunks
    levels = len(radices)
    local = min(2, levels)
    most = max(radices) - 1
    scaling = (depth * size) ** (-0.5)
    dims = tuple(reversed(radices))
    sums, landed = [], []
    for level in range(local, levels):
        high = tuple(reversed(radices[level + 1 :]))
        sums.append(pltpu.VMEM((chunks,) + high + (radices[level], rows, width), BF16))
        landed.append(pltpu.VMEM((chunks, radices[level] - 1) + high + (rows, width), BF16))
    outer_dims, local_dims = dims[: levels - local], dims[levels - local :]
    group = 1
    for radix in local_dims:
        group *= radix
    any_place = pl.BlockSpec(memory_space=pl.ANY)
    dma = pltpu.SemaphoreType.DMA
    return pl.pallas_call(
        functools.partial(kernel, radices, local, replicas, chunks, mixing, scaling),
        out_shape=(
            jax.ShapeDtypeStruct((rows, wide), BF16),
            jax.ShapeDtypeStruct((tokens, depth), BF16),
            jax.ShapeDtypeStruct((depth, wide), BF16),
            jax.ShapeDtypeStruct((depth, wide), BF16),
        ),
        in_specs=[
            any_place,
            any_place,
            any_place,
            pl.BlockSpec(memory_space=pltpu.VMEM),
            any_place,
        ],
        out_specs=(any_place,) * 4,
        scratch_shapes=sums
        + landed
        + [
            pltpu.VMEM(dims + (rows, depth), BF16),
            pltpu.VMEM(local_dims + outer_dims + (rows, depth), BF16),
            pltpu.VMEM((chunks,) + local_dims + (depth, width), BF16),
            pltpu.VMEM((depth, wide), BF16),
            pltpu.VMEM((rows, wide), BF16),
            pltpu.VMEM((chunks,) + dims + (rows, width), BF16),
            pltpu.VMEM((chunks, depth, width), BF16),
            pltpu.VMEM((chunks, depth, width), BF16),
            pltpu.VMEM((depth, wide), BF16),
            pltpu.VMEM((depth, tokens), BF16),
            pltpu.VMEM((tokens, depth), F32),
            pltpu.VMEM((chunks, rows, width), BF16),
            pltpu.VMEM((tokens, depth), BF16),
            pltpu.VMEM((chunks, depth, width), BF16),
            pltpu.VMEM((chunks, depth, width), BF16),
            dma((3,)),
            dma((chunks,)),
            dma((3 * chunks + 1,)),
            dma((group,)),
            dma((group,)),
            dma((levels, chunks, most)),
            dma((levels, chunks, most)),
            dma((levels, chunks, most)),
            dma((levels, chunks, most)),
            dma((levels, chunks, most)),
            dma((levels, chunks, most)),
            dma((chunks + 1,)),
            dma((chunks + 1,)),
        ],
        cost_estimate=pl.CostEstimate(
            flops=6 * tokens * depth * wide, bytes_accessed=8 * depth * wide, transcendentals=0
        ),
        compiler_params=pltpu.CompilerParams(
            collective_id=0, has_side_effects=True, vmem_limit_bytes=VMEM_BYTES
        ),
    )(attn.reshape(dims + (rows, depth)), proj, mom, seg, target)


def passed_along(x, axis, by):
    size = lax.axis_size(axis)
    return lax.ppermute(x, axis, [(i, (i + by) % size) for i in range(size)])


def on_device(attn_out, proj, momentum, target, segment_ids, step):
    tensor_size = lax.axis_size("tensor")
    replicas = lax.axis_size("replica")
    rows_each = target.shape[1] // tensor_size
    bits = replicas.bit_length() - 1
    projected, attn_grad, updated, moment = fused(
        attn_out[0],
        proj[0],
        momentum[0],
        segment_ids,
        target[0].reshape(tensor_size, rows_each, target.shape[2]),
        radices_of(tensor_size),
        replicas,
        replicas == 2,
    )
    if replicas > 2:
        stacked = jnp.stack((updated, moment))
        branches = [
            partial(passed_along, axis="replica", by=1 << bit_pos) for bit_pos in range(bits)
        ]
        partner = lax.switch(step[0] % bits, branches, stacked)
        mixed = ((stacked.astype(F32) + partner.astype(F32)) * 0.5).astype(BF16)
        updated, moment = mixed[0], mixed[1]
    return (projected[None], attn_grad[None], updated[None], moment[None])


def solution(mesh):
    return jax.shard_map(
        on_device,
        mesh=mesh,
        in_specs=(
            P("replica", None, "tensor"),
            P("replica", "tensor", None),
            P("replica", "tensor", None),
            P("replica", None, None),
            P("replica", None),
            P(),
        ),
        out_specs=(
            P("replica", "tensor", None),
            P("replica", None, "tensor"),
            P("replica", "tensor", None),
            P("replica", "tensor", None),
        ),
        check_vma=False,
    )
```

```python
import functools
import itertools
from functools import partial

import jax
import jax.numpy as jnp
from jax import lax
from jax.experimental import pallas as pl
from jax.experimental.pallas import tpu as pltpu
from jax.sharding import PartitionSpec as P

SEGS = 96
BETA_MOM = 0.9
STEP_RATE = 0.1
CHUNKS = 8
HOP_US = 1.5
LINK_GB = 100.0
VMEM_BYTES = 52 * 1024 * 1024
BF16 = jnp.bfloat16
F32 = jnp.float32
MESH = pl.DeviceIdType.MESH


def radices_of(size):
    found = []
    while size > 2 and size % 2 == 0:
        found.append(2)
        size //= 2
    if size > 1:
        found.append(size)
    return tuple(found)


def hops_of(radices, local, replicas, chunks, rows, depth, width):
    levels = len(radices)
    block = 2e-6 * rows * width / LINK_GB
    weight = 2e-6 * depth * width / LINK_GB
    hops = []

    def add(level, time, work):
        chip = level > 0
        hops.append((level, 1e3 * time * (2 if chip else 1 / 6), work))

    for level in range(local - 1, -1, -1):
        held = 1
        for radix in radices[level + 1 : local]:
            held *= radix
        add(level, weight * held, 0.2)
    size = 1
    for radix in radices[local:]:
        size *= radix
    for level in range(local, levels):
        size //= radices[level]
        far = min(2, level - local + 1)
        add(level if level == local else local, block * size * far, 0.3)
    held = 1
    for level in range(levels - 1, -1, -1):
        far = 2 if level > local else 1
        add(min(level, local), block * held * far, 0.3)
        held *= radices[level]
    hops.append(("y", 2e3 * weight, 0.6))
    return hops


def order_of(hops, chunks):
    free, now, order = {}, 0.0, []
    ready = {(0, k): 0.0 for k in range(chunks)}
    while ready:
        task = min(ready, key=lambda at: (max(ready[at], now), -at[0] if at[0] else 1, at[1]))
        stage, k = task
        now = max(now, ready.pop(task))
        order.append(task)
        if stage < len(hops):
            link, time, work = hops[stage]
            now += work
            begin = max(now, free.get(link, 0.0))
            free[link] = begin + time
            ready[stage + 1, k] = begin + time + HOP_US
        else:
            now += 0.3
    return order


def kernel(
    radices,
    local,
    replicas,
    chunks,
    mixing,
    scaling,
    attn_hbm,
    proj_hbm,
    mom_hbm,
    seg_ref,
    target_hbm,
    projected_hbm,
    attn_grad_hbm,
    out_proj_hbm,
    out_mom_hbm,
    *scratch,
):
    levels = len(radices)
    outer = levels - local
    sums = scratch[:outer]
    landed = scratch[outer : 2 * outer]
    (
        attn,
        attn_group,
        proj,
        mom,
        target,
        grads,
        moments,
        partner_moments,
        partner_proj,
        attn_t,
        total,
        projected,
        attn_grad,
        out_proj,
        out_mom,
        in_sem,
        proj_sem,
        out_sem,
        a_send,
        a_recv,
        p_send,
        p_recv,
        rs_send,
        rs_recv,
        ag_send,
        ag_recv,
        y_send,
        y_recv,
    ) = scratch[2 * outer :]
    rows, depth = attn.shape[-2:]
    width = proj.shape[-1]
    me = lax.axis_index("tensor")
    rep = lax.axis_index("replica")
    digits, strides, rest, stride = [], [], me, 1
    for radix in radices:
        digits.append(lax.rem(rest, radix))
        strides.append(stride)
        rest = lax.div(rest, radix)
        stride *= radix
    tokens = stride * rows
    mine = tuple(reversed(digits))
    own = tuple(reversed(digits[:local]))
    outer_all = (slice(None),) * outer

    def peer(level, by):
        to = lax.rem(digits[level] + by, radices[level])
        return to, me + (to - digits[level]) * strides[level]

    group = []
    for offsets in itertools.product(*[range(r) for r in reversed(radices[:local])]):
        if any(offsets):
            there, index = [], me
            for level, by in zip(range(local - 1, -1, -1), offsets):
                to, _ = peer(level, by)
                there.append(to)
                index = index + (to - digits[level]) * strides[level]
            group.append((tuple(there), index))

    other = {"replica": lax.rem(rep + 1, replicas)}

    def columns(k):
        return slice(k * width, (k + 1) * width)

    loads = [
        pltpu.make_async_copy(attn_hbm, attn, in_sem.at[0]),
        pltpu.make_async_copy(mom_hbm, mom, in_sem.at[1]),
        pltpu.make_async_copy(target_hbm.at[me], target, in_sem.at[2]),
    ]
    proj_loads = [
        pltpu.make_async_copy(proj_hbm.at[:, columns(k)], proj.at[(k,) + own], proj_sem.at[k])
        for k in range(chunks)
    ]
    loads[0].start()
    for load in proj_loads:
        load.start()
    loads[1].start()
    loads[2].start()

    barrier = pltpu.get_barrier_semaphore()
    greet = [{"tensor": index} for _, index in group]
    for level in range(local, levels):
        greet += [{"tensor": peer(level, by)[1]} for by in range(1, radices[level])]
    if mixing:
        greet.append(other)
    for device in greet:
        pl.semaphore_signal(barrier, inc=1, device_id=device, device_id_type=MESH)
    loads[0].wait()
    pl.semaphore_wait(barrier, len(greet))

    copies = {}

    def send(key, src, dst, send_sem, recv_sem, device):
        copy = pltpu.make_async_remote_copy(
            src_ref=src,
            dst_ref=dst,
            send_sem=send_sem,
            recv_sem=recv_sem,
            device_id=device,
            device_id_type=MESH,
        )
        copy.start()
        copies[key] = copy

    for i, (there, index) in enumerate(group):
        send(
            ("a", i),
            attn.at[outer_all + there],
            attn_group.at[own],
            a_send.at[i],
            a_recv.at[i],
            {"tensor": index},
        )

    def gather(kind, ref, sems, level, k, high):
        place = (k,) + high + tuple(digits[i] for i in range(level, -1, -1))
        for by in range(1, radices[level]):
            send(
                (kind, level, k, by),
                ref.at[place],
                ref.at[place],
                sems[0].at[level, k, by - 1],
                sems[1].at[level, k, by - 1],
                {"tensor": peer(level, by)[1]},
            )

    def share_proj(level, k):
        gather("p", proj, (p_send, p_recv), level, k, (slice(None),) * (local - 1 - level))

    def share_grad(level, k):
        gather("g", grads, (ag_send, ag_recv), level, k, (slice(None),) * (levels - 1 - level))

    def reduce_start(level, k):
        high = (slice(None),) * (levels - 1 - level)
        for by in range(1, radices[level]):
            to, index = peer(level, by)
            send(
                ("r", level, k, by),
                sums[level - local].at[(k,) + high + (to,)],
                landed[level - local].at[k, by - 1],
                rs_send.at[level, k, by - 1],
                rs_recv.at[level, k, by - 1],
                {"tensor": index},
            )

    def wait_recv(kind, level, k):
        for by in range(1, radices[level]):
            copies[kind, level, k, by].wait_recv()

    def first(k):
        proj_loads[k].wait()
        if local > 0:
            share_proj(local - 1, k)

    def proj_stage(level, k):
        wait_recv("p", level, k)
        share_proj(level - 1, k)

    def product(k):
        if local > 0:
            wait_recv("p", 0, k)
        if k == 0:
            for i in range(len(group)):
                copies["a", i].wait_recv()
        part = jnp.zeros((tokens // len_group, width), F32)
        for at in itertools.product(*[range(r) for r in reversed(radices[:local])]):
            left = attn_group[at]
            part = part + jnp.dot(flat(left), proj[(k,) + at], preferred_element_type=F32)
        shape = tuple(reversed(radices[local:])) + (rows, width)
        part = part.reshape(shape)
        if outer > 0:
            sums[0][k] = part.astype(BF16)
            reduce_start(local, k)
        else:
            finish(part, k)

    def flat(block):
        count = 1
        for n in block.shape[:-1]:
            count *= n
        if rows % 16:
            return block.astype(F32).reshape(count, block.shape[-1]).astype(BF16)
        return block.reshape(count, block.shape[-1])

    def reduce_stage(level, k):
        wait_recv("r", level, k)
        high = (slice(None),) * (levels - 1 - level)
        value = sums[level - local][(k,) + high + (digits[level],)].astype(F32)
        for by in range(1, radices[level]):
            value = value + landed[level - local][k, by - 1].astype(F32)
        if level + 1 < levels:
            sums[level + 1 - local][k] = value.astype(BF16)
            reduce_start(level + 1, k)
        else:
            finish(value, k)

    def finish(value, k):
        if k == 0:
            loads[2].wait()
        summed = value * scaling
        grad = (summed - target[:, columns(k)].astype(F32)) * weights
        grads[(k,) + mine] = grad.astype(BF16)
        share_grad(levels - 1, k)
        projected[k] = summed.astype(BF16)
        store(("projected", k), projected.at[k], projected_hbm.at[:, columns(k)], 3 * k)

    stores = []

    def store(key, src, dst, place):
        copy = pltpu.make_async_copy(src, dst, out_sem.at[place])
        copy.start()
        stores.append(copy)

    def gather_stage(level, k):
        wait_recv("g", level, k)
        if level > 0:
            share_grad(level - 1, k)
            return
        if k == 0:
            loads[1].wait()
        block = flat(grads[k])
        weight = proj[(k,) + own]
        gradient = jnp.dot(attn_t[...], block, preferred_element_type=F32) * scaling
        moment = (BETA_MOM * mom[:, columns(k)].astype(F32) + gradient).astype(BF16)
        if mixing:
            moments[k] = moment
            send(
                ("y", k),
                moments.at[k],
                partner_moments.at[k],
                y_send.at[k],
                y_recv.at[k],
                other,
            )
        else:
            put(k, updated_of(weight, moment), moment)
        total[...] += lax.dot_general(
            block, weight, (((1,), (1,)), ((), ())), preferred_element_type=F32
        )

    def put(k, new_proj, new_moment):
        out_proj[k] = new_proj
        out_mom[k] = new_moment
        store(("proj", k), out_proj.at[k], out_proj_hbm.at[:, columns(k)], 3 * k + 1)
        store(("mom", k), out_mom.at[k], out_mom_hbm.at[:, columns(k)], 3 * k + 2)

    def updated_of(weight, moment):
        return (weight.astype(F32) - STEP_RATE * moment.astype(F32)).astype(BF16)

    def mix_stage(k):
        if not mixing:
            return
        if k == 0:
            copies["yp"].wait_recv()
        copies["y", k].wait_recv()
        ours, theirs = moments[k], partner_moments[k]
        one = updated_of(proj[(k,) + own], ours).astype(F32)
        two = updated_of(partner_proj[:, columns(k)], theirs).astype(F32)
        put(
            k,
            ((one + two) * 0.5).astype(BF16),
            ((ours.astype(F32) + theirs.astype(F32)) * 0.5).astype(BF16),
        )

    len_group = len(group) + 1
    stages = [first]
    stages += [partial(proj_stage, level) for level in range(local - 1, 0, -1)]
    stages += [product]
    stages += [partial(reduce_stage, level) for level in range(local, levels)]
    stages += [partial(gather_stage, level) for level in range(levels - 1, -1, -1)]
    stages += [mix_stage]

    order = order_of(hops_of(radices, local, replicas, chunks, rows, depth, width), chunks)
    ahead = 0
    while ahead < len(order) and order[ahead][0] == 0:
        first(order[ahead][1])
        ahead += 1
    if mixing:
        send(
            "yp",
            proj_hbm,
            partner_proj,
            y_send.at[chunks],
            y_recv.at[chunks],
            other,
        )
    attn_group[own] = attn[outer_all + own]

    seg = seg_ref[...].astype(F32)
    shape = (rows, tokens)
    row_at = lax.broadcasted_iota(jnp.int32, shape, 0) + me * rows
    col_at = lax.broadcasted_iota(jnp.int32, shape, 1)
    seg_all = jnp.broadcast_to(seg, shape)
    own_seg = jnp.sum(jnp.where(row_at == col_at, seg_all, 0.0), axis=1, keepdims=True)
    count = jnp.sum(jnp.where(seg_all == own_seg, 1.0, 0.0), axis=1, keepdims=True)
    weights = tokens / (SEGS * count)
    attn_t[...] = flat(attn[...]).T
    total[...] = jnp.zeros_like(total)

    for j, k in order[ahead:]:
        stages[j](k)

    attn_grad[...] = (total[...] * scaling).astype(BF16)
    store("attn_grad", attn_grad, attn_grad_hbm, 3 * chunks)
    for copy in copies.values():
        copy.wait_send()
    for copy in stores:
        copy.wait()


def fused(attn, proj, mom, seg, target, radices, replicas, mixing):
    size, rows, wide = target.shape
    tokens, depth = size * rows, proj.shape[0]
    chunks = CHUNKS
    width = wide // chunks
    levels = len(radices)
    local = min(2, levels)
    most = max(radices) - 1
    scaling = (depth * size) ** (-0.5)
    dims = tuple(reversed(radices))
    sums, landed = [], []
    for level in range(local, levels):
        high = tuple(reversed(radices[level + 1 :]))
        sums.append(pltpu.VMEM((chunks,) + high + (radices[level], rows, width), BF16))
        landed.append(pltpu.VMEM((chunks, radices[level] - 1) + high + (rows, width), BF16))
    outer_dims, local_dims = dims[: levels - local], dims[levels - local :]
    group = 1
    for radix in local_dims:
        group *= radix
    any_place = pl.BlockSpec(memory_space=pl.ANY)
    dma = pltpu.SemaphoreType.DMA
    return pl.pallas_call(
        functools.partial(kernel, radices, local, replicas, chunks, mixing, scaling),
        out_shape=(
            jax.ShapeDtypeStruct((rows, wide), BF16),
            jax.ShapeDtypeStruct((tokens, depth), BF16),
            jax.ShapeDtypeStruct((depth, wide), BF16),
            jax.ShapeDtypeStruct((depth, wide), BF16),
        ),
        in_specs=[
            any_place,
            any_place,
            any_place,
            pl.BlockSpec(memory_space=pltpu.VMEM),
            any_place,
        ],
        out_specs=(any_place,) * 4,
        scratch_shapes=sums
        + landed
        + [
            pltpu.VMEM(dims + (rows, depth), BF16),
            pltpu.VMEM(local_dims + outer_dims + (rows, depth), BF16),
            pltpu.VMEM((chunks,) + local_dims + (depth, width), BF16),
            pltpu.VMEM((depth, wide), BF16),
            pltpu.VMEM((rows, wide), BF16),
            pltpu.VMEM((chunks,) + dims + (rows, width), BF16),
            pltpu.VMEM((chunks, depth, width), BF16),
            pltpu.VMEM((chunks, depth, width), BF16),
            pltpu.VMEM((depth, wide), BF16),
            pltpu.VMEM((depth, tokens), BF16),
            pltpu.VMEM((tokens, depth), F32),
            pltpu.VMEM((chunks, rows, width), BF16),
            pltpu.VMEM((tokens, depth), BF16),
            pltpu.VMEM((chunks, depth, width), BF16),
            pltpu.VMEM((chunks, depth, width), BF16),
            dma((3,)),
            dma((chunks,)),
            dma((3 * chunks + 1,)),
            dma((group,)),
            dma((group,)),
            dma((levels, chunks, most)),
            dma((levels, chunks, most)),
            dma((levels, chunks, most)),
            dma((levels, chunks, most)),
            dma((levels, chunks, most)),
            dma((levels, chunks, most)),
            dma((chunks + 1,)),
            dma((chunks + 1,)),
        ],
        cost_estimate=pl.CostEstimate(
            flops=6 * tokens * depth * wide, bytes_accessed=8 * depth * wide, transcendentals=0
        ),
        compiler_params=pltpu.CompilerParams(
            collective_id=0, has_side_effects=True, vmem_limit_bytes=VMEM_BYTES
        ),
    )(attn.reshape(dims + (rows, depth)), proj, mom, seg, target)


def passed_along(x, axis, by):
    size = lax.axis_size(axis)
    return lax.ppermute(x, axis, [(i, (i + by) % size) for i in range(size)])


def on_device(attn_out, proj, momentum, target, segment_ids, step):
    tensor_size = lax.axis_size("tensor")
    replicas = lax.axis_size("replica")
    rows_each = target.shape[1] // tensor_size
    bits = replicas.bit_length() - 1
    projected, attn_grad, updated, moment = fused(
        attn_out[0],
        proj[0],
        momentum[0],
        segment_ids,
        target[0].reshape(tensor_size, rows_each, target.shape[2]),
        radices_of(tensor_size),
        replicas,
        replicas == 2,
    )
    if replicas > 2:
        stacked = jnp.stack((updated, moment))
        branches = [
            partial(passed_along, axis="replica", by=1 << bit_pos) for bit_pos in range(bits)
        ]
        partner = lax.switch(step[0] % bits, branches, stacked)
        mixed = ((stacked.astype(F32) + partner.astype(F32)) * 0.5).astype(BF16)
        updated, moment = mixed[0], mixed[1]
    return (projected[None], attn_grad[None], updated[None], moment[None])


def solution(mesh):
    return jax.shard_map(
        on_device,
        mesh=mesh,
        in_specs=(
            P("replica", None, "tensor"),
            P("replica", "tensor", None),
            P("replica", "tensor", None),
            P("replica", None, None),
            P("replica", None),
            P(),
        ),
        out_specs=(
            P("replica", "tensor", None),
            P("replica", None, "tensor"),
            P("replica", "tensor", None),
            P("replica", "tensor", None),
        ),
        check_vma=False,
    )
```

```python
import functools
import itertools
from functools import partial

import jax
import jax.numpy as jnp
from jax import lax
from jax.experimental import pallas as pl
from jax.experimental.pallas import tpu as pltpu
from jax.sharding import PartitionSpec as P

SEGS = 96
BETA_MOM = 0.9
STEP_RATE = 0.1
CHUNKS = 8
HOP_US = 1.5
LINK_GB = 100.0
VMEM_BYTES = 52 * 1024 * 1024
BF16 = jnp.bfloat16
F32 = jnp.float32
MESH = pl.DeviceIdType.MESH


def radices_of(size):
    found = []
    while size > 2 and size % 2 == 0:
        found.append(2)
        size //= 2
    if size > 1:
        found.append(size)
    return tuple(found)


def hops_of(radices, local, replicas, chunks, rows, depth, width):
    levels = len(radices)
    block = 2e-3 * rows * width / LINK_GB
    weight = 2e-3 * depth * width / LINK_GB
    outer = 1
    for radix in radices[local:]:
        outer *= radix
    hops, held = [], 1
    for level in range(local - 1, -1, -1):
        time = weight * held
        hops.append((level, time * 2 if level else time / 6, 0.2))
        held *= radices[level]
    hops.append(("far", 2 * block * max(1, outer - 1) * 4 / 3, 0.6))
    held = 1
    for level in range(levels - 1, -1, -1):
        time = block * held
        if level >= local:
            last = level == levels - 1
            hops.append(("far" if last else local, time * (4 if last else 2), 0.4 if last else 0.2))
        else:
            hops.append((level, time * 2 if level else time / 6, 0.2))
        held *= radices[level]
    hops.append(("y", 2 * weight, 0.8))
    return hops


def order_of(hops, chunks):
    free, now, order = {}, 0.0, []
    ready = {(0, k): 0.0 for k in range(chunks)}
    while ready:
        task = min(ready, key=lambda at: (max(ready[at], now), -at[0] if at[0] else 1, at[1]))
        stage, k = task
        now = max(now, ready.pop(task))
        order.append(task)
        if stage < len(hops):
            link, time, work = hops[stage]
            now += work
            begin = max(now, free.get(link, 0.0))
            free[link] = begin + time
            ready[stage + 1, k] = begin + time + HOP_US
        else:
            now += 0.3
    return order


def kernel(
    radices,
    local,
    replicas,
    chunks,
    mixing,
    scaling,
    attn_hbm,
    proj_hbm,
    mom_hbm,
    seg_ref,
    target_hbm,
    projected_ref,
    attn_grad_ref,
    out_proj_ref,
    out_mom_ref,
    *scratch,
):
    levels = len(radices)
    outer = levels - local
    (
        sums,
        landed,
        attn,
        attn_group,
        proj,
        mom,
        target,
        grads,
        moments,
        partner_moments,
        partner_proj,
        attn_t,
        total,
        in_sem,
        proj_sem,
        a_send,
        a_recv,
        p_send,
        p_recv,
        rs_send,
        rs_recv,
        ag_send,
        ag_recv,
        y_send,
        y_recv,
    ) = scratch
    rows, depth = attn.shape[-2:]
    width = proj.shape[-1]
    me = lax.axis_index("tensor")
    rep = lax.axis_index("replica")
    digits, strides, rest, stride = [], [], me, 1
    for radix in radices:
        digits.append(lax.rem(rest, radix))
        strides.append(stride)
        rest = lax.div(rest, radix)
        stride *= radix
    tokens = stride * rows
    mine = tuple(reversed(digits))
    own = tuple(reversed(digits[:local]))
    outer_all = (slice(None),) * outer

    def peer(level, by):
        to = lax.rem(digits[level] + by, radices[level])
        return to, me + (to - digits[level]) * strides[level]

    def others(levels_of):
        found = []
        for offsets in itertools.product(*[range(radices[level]) for level in levels_of]):
            if any(offsets):
                there, index = [], me
                for level, by in zip(levels_of, offsets):
                    to, _ = peer(level, by)
                    there.append(to)
                    index = index + (to - digits[level]) * strides[level]
                found.append((tuple(there), index))
        return found

    group = others(range(local - 1, -1, -1))
    summers = others(range(levels - 1, local - 1, -1))

    other = {"replica": lax.rem(rep + 1, replicas)}

    def columns(k):
        return slice(k * width, (k + 1) * width)

    loads = [
        pltpu.make_async_copy(attn_hbm, attn, in_sem.at[0]),
        pltpu.make_async_copy(mom_hbm, mom, in_sem.at[1]),
        pltpu.make_async_copy(target_hbm.at[me], target, in_sem.at[2]),
    ]
    proj_loads = [
        pltpu.make_async_copy(proj_hbm.at[:, columns(k)], proj.at[(k,) + own], proj_sem.at[k])
        for k in range(chunks)
    ]
    loads[0].start()
    for load in proj_loads:
        load.start()
    loads[1].start()
    loads[2].start()

    barrier = pltpu.get_barrier_semaphore()
    greet = [{"tensor": index} for _, index in group]
    greet += [{"tensor": index} for _, index in summers]
    if mixing:
        greet.append(other)
    for device in greet:
        pl.semaphore_signal(barrier, inc=1, device_id=device, device_id_type=MESH)
    pl.semaphore_wait(barrier, len(greet))

    copies = {}

    def send(key, src, dst, send_sem, recv_sem, device):
        copy = pltpu.make_async_remote_copy(
            src_ref=src,
            dst_ref=dst,
            send_sem=send_sem,
            recv_sem=recv_sem,
            device_id=device,
            device_id_type=MESH,
        )
        copy.start()
        copies[key] = copy

    for i, (there, index) in enumerate(group):
        send(
            ("a", i),
            attn_hbm.at[outer_all + there],
            attn_group.at[own],
            a_send.at[i],
            a_recv.at[i],
            {"tensor": index},
        )

    def gather(kind, ref, sems, level, k, high):
        place = (k,) + high + tuple(digits[i] for i in range(level, -1, -1))
        for by in range(1, radices[level]):
            send(
                (kind, level, k, by),
                ref.at[place],
                ref.at[place],
                sems[0].at[level, k, by - 1],
                sems[1].at[level, k, by - 1],
                {"tensor": peer(level, by)[1]},
            )

    def share_proj(level, k):
        if level == local - 1:
            place = (k,) + own
            for by in range(1, radices[level]):
                send(
                    ("p", level, k, by),
                    proj_hbm.at[:, columns(k)],
                    proj.at[place],
                    p_send.at[level, k, by - 1],
                    p_recv.at[level, k, by - 1],
                    {"tensor": peer(level, by)[1]},
                )
            return
        gather("p", proj, (p_send, p_recv), level, k, (slice(None),) * (local - 1 - level))

    def share_grad(level, k):
        gather("g", grads, (ag_send, ag_recv), level, k, (slice(None),) * (levels - 1 - level))

    def reduce_start(k):
        for i, (there, index) in enumerate(summers):
            send(
                ("r", i, k),
                sums.at[(k,) + there],
                landed.at[k, i],
                rs_send.at[i, k],
                rs_recv.at[i, k],
                {"tensor": index},
            )

    def wait_recv(kind, level, k):
        for by in range(1, radices[level]):
            copies[kind, level, k, by].wait_recv()

    def first(k):
        if local > 0:
            share_proj(local - 1, k)

    def proj_stage(level, k):
        proj_loads[k].wait()
        wait_recv("p", level, k)
        share_proj(level - 1, k)

    def product(k):
        if local < 2:
            proj_loads[k].wait()
        if local > 0:
            wait_recv("p", 0, k)
        if k == 0:
            for i in range(len(group)):
                copies["a", i].wait_recv()
        part = jnp.zeros((tokens // len_group, width), F32)
        for at in itertools.product(*[range(r) for r in reversed(radices[:local])]):
            left = attn_group[at]
            part = part + jnp.dot(flat(left), proj[(k,) + at], preferred_element_type=F32)
        shape = tuple(reversed(radices[local:])) + (rows, width)
        part = part.reshape(shape)
        sums[k] = part.astype(BF16)
        reduce_start(k)

    def flat(block):
        count = 1
        for n in block.shape[:-1]:
            count *= n
        if rows % 16:
            return block.astype(F32).reshape(count, block.shape[-1]).astype(BF16)
        return block.reshape(count, block.shape[-1])

    def reduce_stage(k):
        value = sums[(k,) + mine[:outer]].astype(F32)
        for i in range(len(summers)):
            copies["r", i, k].wait_recv()
            value = value + landed[k, i].astype(F32)
        finish(value, k)

    def finish(value, k):
        if k == 0:
            loads[2].wait()
        summed = value * scaling
        grad = (summed - target[:, columns(k)].astype(F32)) * weights
        grads[(k,) + mine] = grad.astype(BF16)
        share_grad(levels - 1, k)
        projected_ref[:, columns(k)] = summed.astype(BF16)

    def gather_stage(level, k):
        wait_recv("g", level, k)
        if level > 0:
            share_grad(level - 1, k)
            return
        if k == 0:
            loads[1].wait()
        block = flat(grads[k])
        weight = proj[(k,) + own]
        gradient = jnp.dot(attn_t[...], block, preferred_element_type=F32) * scaling
        moment = (BETA_MOM * mom[:, columns(k)].astype(F32) + gradient).astype(BF16)
        if mixing:
            moments[k] = moment
            send(
                ("y", k),
                moments.at[k],
                partner_moments.at[k],
                y_send.at[k],
                y_recv.at[k],
                other,
            )
        else:
            put(k, updated_of(weight, moment), moment)
        total[...] += lax.dot_general(
            block, weight, (((1,), (1,)), ((), ())), preferred_element_type=F32
        )

    def put(k, new_proj, new_moment):
        out_proj_ref[:, columns(k)] = new_proj
        out_mom_ref[:, columns(k)] = new_moment

    def updated_of(weight, moment):
        return (weight.astype(F32) - STEP_RATE * moment.astype(F32)).astype(BF16)

    def mix_stage(k):
        if not mixing:
            return
        if k == 0:
            copies["yp"].wait_recv()
        copies["y", k].wait_recv()
        ours, theirs = moments[k], partner_moments[k]
        one = updated_of(proj[(k,) + own], ours).astype(F32)
        two = updated_of(partner_proj[:, columns(k)], theirs).astype(F32)
        put(
            k,
            ((one + two) * 0.5).astype(BF16),
            ((ours.astype(F32) + theirs.astype(F32)) * 0.5).astype(BF16),
        )

    len_group = len(group) + 1
    stages = [first]
    stages += [partial(proj_stage, level) for level in range(local - 1, 0, -1)]
    stages += [product]
    stages += [reduce_stage]
    stages += [partial(gather_stage, level) for level in range(levels - 1, -1, -1)]
    stages += [mix_stage]

    order = order_of(hops_of(radices, local, replicas, chunks, rows, depth, width), chunks)
    ahead = 0
    while ahead < len(order) and order[ahead][0] == 0:
        first(order[ahead][1])
        ahead += 1
    if mixing:
        send(
            "yp",
            proj_hbm,
            partner_proj,
            y_send.at[chunks],
            y_recv.at[chunks],
            other,
        )
    loads[0].wait()
    attn_group[own] = attn[outer_all + own]

    seg = seg_ref[...].astype(F32)
    shape = (rows, tokens)
    row_at = lax.broadcasted_iota(jnp.int32, shape, 0) + me * rows
    col_at = lax.broadcasted_iota(jnp.int32, shape, 1)
    seg_all = jnp.broadcast_to(seg, shape)
    own_seg = jnp.sum(jnp.where(row_at == col_at, seg_all, 0.0), axis=1, keepdims=True)
    count = jnp.sum(jnp.where(seg_all == own_seg, 1.0, 0.0), axis=1, keepdims=True)
    weights = tokens / (SEGS * count)
    attn_t[...] = flat(attn[...]).T
    total[...] = jnp.zeros_like(total)

    for j, k in order[ahead:]:
        stages[j](k)

    attn_grad_ref[...] = (total[...] * scaling).astype(BF16)
    for copy in copies.values():
        copy.wait_send()


def fused(attn, proj, mom, seg, target, radices, replicas, mixing):
    size, rows, wide = target.shape
    tokens, depth = size * rows, proj.shape[0]
    chunks = CHUNKS
    width = wide // chunks
    levels = len(radices)
    local = min(2, levels)
    most = max(radices) - 1
    scaling = (depth * size) ** (-0.5)
    dims = tuple(reversed(radices))
    outer_dims, local_dims = dims[: levels - local], dims[levels - local :]
    group = 1
    for radix in local_dims:
        group *= radix
    summers = size // group - 1
    vmem = pl.BlockSpec(memory_space=pltpu.VMEM)
    any_place = pl.BlockSpec(memory_space=pl.ANY)
    dma = pltpu.SemaphoreType.DMA
    return pl.pallas_call(
        functools.partial(kernel, radices, local, replicas, chunks, mixing, scaling),
        out_shape=(
            jax.ShapeDtypeStruct((rows, wide), BF16),
            jax.ShapeDtypeStruct((tokens, depth), BF16),
            jax.ShapeDtypeStruct((depth, wide), BF16),
            jax.ShapeDtypeStruct((depth, wide), BF16),
        ),
        in_specs=[
            any_place,
            any_place,
            any_place,
            vmem,
            any_place,
        ],
        out_specs=(vmem,) * 4,
        scratch_shapes=[
            pltpu.VMEM((chunks,) + outer_dims + (rows, width), BF16),
            pltpu.VMEM((chunks, max(1, summers), rows, width), BF16),
            pltpu.VMEM(dims + (rows, depth), BF16),
            pltpu.VMEM(local_dims + outer_dims + (rows, depth), BF16),
            pltpu.VMEM((chunks,) + local_dims + (depth, width), BF16),
            pltpu.VMEM((depth, wide), BF16),
            pltpu.VMEM((rows, wide), BF16),
            pltpu.VMEM((chunks,) + dims + (rows, width), BF16),
            pltpu.VMEM((chunks, depth, width), BF16),
            pltpu.VMEM((chunks, depth, width), BF16),
            pltpu.VMEM((depth, wide), BF16),
            pltpu.VMEM((depth, tokens), BF16),
            pltpu.VMEM((tokens, depth), F32),
            dma((3,)),
            dma((chunks,)),
            dma((group,)),
            dma((group,)),
            dma((levels, chunks, most)),
            dma((levels, chunks, most)),
            dma((max(1, summers), chunks)),
            dma((max(1, summers), chunks)),
            dma((levels, chunks, most)),
            dma((levels, chunks, most)),
            dma((chunks + 1,)),
            dma((chunks + 1,)),
        ],
        cost_estimate=pl.CostEstimate(
            flops=6 * tokens * depth * wide, bytes_accessed=8 * depth * wide, transcendentals=0
        ),
        compiler_params=pltpu.CompilerParams(
            collective_id=0, has_side_effects=True, vmem_limit_bytes=VMEM_BYTES
        ),
    )(attn.reshape(dims + (rows, depth)), proj, mom, seg, target)


def passed_along(x, axis, by):
    size = lax.axis_size(axis)
    return lax.ppermute(x, axis, [(i, (i + by) % size) for i in range(size)])


def on_device(attn_out, proj, momentum, target, segment_ids, step):
    tensor_size = lax.axis_size("tensor")
    replicas = lax.axis_size("replica")
    rows_each = target.shape[1] // tensor_size
    bits = replicas.bit_length() - 1
    projected, attn_grad, updated, moment = fused(
        attn_out[0],
        proj[0],
        momentum[0],
        segment_ids,
        target[0].reshape(tensor_size, rows_each, target.shape[2]),
        radices_of(tensor_size),
        replicas,
        replicas == 2,
    )
    if replicas > 2:
        stacked = jnp.stack((updated, moment))
        branches = [
            partial(passed_along, axis="replica", by=1 << bit_pos) for bit_pos in range(bits)
        ]
        partner = lax.switch(step[0] % bits, branches, stacked)
        mixed = ((stacked.astype(F32) + partner.astype(F32)) * 0.5).astype(BF16)
        updated, moment = mixed[0], mixed[1]
    return (projected[None], attn_grad[None], updated[None], moment[None])


def solution(mesh):
    return jax.shard_map(
        on_device,
        mesh=mesh,
        in_specs=(
            P("replica", None, "tensor"),
            P("replica", "tensor", None),
            P("replica", "tensor", None),
            P("replica", None, None),
            P("replica", None),
            P(),
        ),
        out_specs=(
            P("replica", "tensor", None),
            P("replica", None, "tensor"),
            P("replica", "tensor", None),
            P("replica", "tensor", None),
        ),
        check_vma=False,
    )
```

```python
import functools
import itertools
from functools import partial

import jax
import jax.numpy as jnp
from jax import lax
from jax.experimental import pallas as pl
from jax.experimental.pallas import tpu as pltpu
from jax.sharding import PartitionSpec as P

SEGS = 96
BETA_MOM = 0.9
STEP_RATE = 0.1
CHUNKS = 8
HOP_US = 1.5
AHEAD = 3
LINK_GB = 100.0
VMEM_BYTES = 52 * 1024 * 1024
BF16 = jnp.bfloat16
F32 = jnp.float32
MESH = pl.DeviceIdType.MESH


def radices_of(size):
    found = []
    while size > 2 and size % 2 == 0:
        found.append(2)
        size //= 2
    if size > 1:
        found.append(size)
    return tuple(found)


def hops_of(radices, local, replicas, chunks, rows, depth, width):
    levels = len(radices)
    block = 2e-6 * rows * width / LINK_GB
    weight = 2e-6 * depth * width / LINK_GB
    hops = []

    def add(level, time, work):
        chip = level > 0
        hops.append((level, 1e3 * time * (2 if chip else 1 / 6), work))

    for level in range(local - 1, -1, -1):
        held = 1
        for radix in radices[level + 1 : local]:
            held *= radix
        add(level, weight * held, 0.2)
    size = 1
    for radix in radices[local:]:
        size *= radix
    for level in range(local, levels):
        size //= radices[level]
        far = min(2, level - local + 1)
        add(level if level == local else local, block * size * far, 0.3)
    held = 1
    for level in range(levels - 1, -1, -1):
        far = 2 if level > local else 1
        add(min(level, local), block * held * far, 0.3)
        held *= radices[level]
    hops.append(("y", 2e3 * weight, 0.6))
    return hops


def order_of(hops, chunks):
    free, now, order = {}, 0.0, []
    ready = {(0, k): 0.0 for k in range(min(AHEAD, chunks))}
    while ready:
        task = min(ready, key=lambda at: (max(ready[at], now), -at[0] if at[0] else 1, at[1]))
        stage, k = task
        now = max(now, ready.pop(task))
        order.append(task)
        if stage == 1 and k + AHEAD < chunks:
            ready[0, k + AHEAD] = now
        if stage < len(hops):
            link, time, work = hops[stage]
            now += work
            begin = max(now, free.get(link, 0.0))
            free[link] = begin + time
            ready[stage + 1, k] = begin + time + HOP_US
        else:
            now += 0.3
    return order


def kernel(
    radices,
    local,
    replicas,
    chunks,
    mixing,
    scaling,
    attn_hbm,
    proj_hbm,
    mom_hbm,
    seg_ref,
    target_hbm,
    projected_ref,
    attn_grad_ref,
    out_proj_ref,
    out_mom_ref,
    *scratch,
):
    levels = len(radices)
    outer = levels - local
    sums = scratch[:outer]
    landed = scratch[outer : 2 * outer]
    (
        attn,
        attn_group,
        proj,
        mom,
        target,
        grads,
        moments,
        partner_moments,
        partner_proj,
        attn_t,
        total,
        in_sem,
        proj_sem,
        a_send,
        a_recv,
        p_send,
        p_recv,
        rs_send,
        rs_recv,
        ag_send,
        ag_recv,
        y_send,
        y_recv,
    ) = scratch[2 * outer :]
    rows, depth = attn.shape[-2:]
    width = proj.shape[-1]
    me = lax.axis_index("tensor")
    rep = lax.axis_index("replica")
    digits, strides, rest, stride = [], [], me, 1
    for radix in radices:
        digits.append(lax.rem(rest, radix))
        strides.append(stride)
        rest = lax.div(rest, radix)
        stride *= radix
    tokens = stride * rows
    mine = tuple(reversed(digits))
    own = tuple(reversed(digits[:local]))
    outer_all = (slice(None),) * outer

    def peer(level, by):
        to = lax.rem(digits[level] + by, radices[level])
        return to, me + (to - digits[level]) * strides[level]

    group = []
    for offsets in itertools.product(*[range(r) for r in reversed(radices[:local])]):
        if any(offsets):
            there, index = [], me
            for level, by in zip(range(local - 1, -1, -1), offsets):
                to, _ = peer(level, by)
                there.append(to)
                index = index + (to - digits[level]) * strides[level]
            group.append((tuple(there), index))

    other = {"replica": lax.rem(rep + 1, replicas)}

    def columns(k):
        return slice(k * width, (k + 1) * width)

    loads = [
        pltpu.make_async_copy(attn_hbm, attn, in_sem.at[0]),
        pltpu.make_async_copy(mom_hbm, mom, in_sem.at[1]),
        pltpu.make_async_copy(target_hbm.at[me], target, in_sem.at[2]),
    ]
    proj_loads = [
        pltpu.make_async_copy(proj_hbm.at[:, columns(k)], proj.at[(k,) + own], proj_sem.at[k])
        for k in range(chunks)
    ]
    loads[0].start()
    for load in proj_loads:
        load.start()
    loads[1].start()
    loads[2].start()

    barrier = pltpu.get_barrier_semaphore()
    greet = [{"tensor": index} for _, index in group]
    for level in range(local, levels):
        greet += [{"tensor": peer(level, by)[1]} for by in range(1, radices[level])]
    if mixing:
        greet.append(other)
    for device in greet:
        pl.semaphore_signal(barrier, inc=1, device_id=device, device_id_type=MESH)
    loads[0].wait()
    pl.semaphore_wait(barrier, len(greet))

    copies = {}

    def send(key, src, dst, send_sem, recv_sem, device):
        copy = pltpu.make_async_remote_copy(
            src_ref=src,
            dst_ref=dst,
            send_sem=send_sem,
            recv_sem=recv_sem,
            device_id=device,
            device_id_type=MESH,
        )
        copy.start()
        copies[key] = copy

    for i, (there, index) in enumerate(group):
        send(
            ("a", i),
            attn.at[outer_all + there],
            attn_group.at[own],
            a_send.at[i],
            a_recv.at[i],
            {"tensor": index},
        )

    def gather(kind, ref, sems, level, k, high):
        place = (k,) + high + tuple(digits[i] for i in range(level, -1, -1))
        for by in range(1, radices[level]):
            send(
                (kind, level, k, by),
                ref.at[place],
                ref.at[place],
                sems[0].at[level, k, by - 1],
                sems[1].at[level, k, by - 1],
                {"tensor": peer(level, by)[1]},
            )

    def share_proj(level, k):
        gather("p", proj, (p_send, p_recv), level, k, (slice(None),) * (local - 1 - level))

    def share_grad(level, k):
        gather("g", grads, (ag_send, ag_recv), level, k, (slice(None),) * (levels - 1 - level))

    def reduce_start(level, k):
        high = (slice(None),) * (levels - 1 - level)
        for by in range(1, radices[level]):
            to, index = peer(level, by)
            send(
                ("r", level, k, by),
                sums[level - local].at[(k,) + high + (to,)],
                landed[level - local].at[k, by - 1],
                rs_send.at[level, k, by - 1],
                rs_recv.at[level, k, by - 1],
                {"tensor": index},
            )

    def wait_recv(kind, level, k):
        for by in range(1, radices[level]):
            copies[kind, level, k, by].wait_recv()

    def first(k):
        proj_loads[k].wait()
        if local > 0:
            share_proj(local - 1, k)

    def proj_stage(level, k):
        wait_recv("p", level, k)
        share_proj(level - 1, k)

    def product(k):
        if local > 0:
            wait_recv("p", 0, k)
        if k == 0:
            for i in range(len(group)):
                copies["a", i].wait_recv()
        part = jnp.zeros((tokens // len_group, width), F32)
        for at in itertools.product(*[range(r) for r in reversed(radices[:local])]):
            left = attn_group[at]
            part = part + jnp.dot(flat(left), proj[(k,) + at], preferred_element_type=F32)
        shape = tuple(reversed(radices[local:])) + (rows, width)
        part = part.reshape(shape)
        if outer > 0:
            sums[0][k] = part.astype(BF16)
            reduce_start(local, k)
        else:
            finish(part, k)

    def flat(block):
        count = 1
        for n in block.shape[:-1]:
            count *= n
        if rows % 16:
            return block.astype(F32).reshape(count, block.shape[-1]).astype(BF16)
        return block.reshape(count, block.shape[-1])

    def reduce_stage(level, k):
        wait_recv("r", level, k)
        high = (slice(None),) * (levels - 1 - level)
        value = sums[level - local][(k,) + high + (digits[level],)].astype(F32)
        for by in range(1, radices[level]):
            value = value + landed[level - local][k, by - 1].astype(F32)
        if level + 1 < levels:
            sums[level + 1 - local][k] = value.astype(BF16)
            reduce_start(level + 1, k)
        else:
            finish(value, k)

    def finish(value, k):
        if k == 0:
            loads[2].wait()
        summed = value * scaling
        grad = (summed - target[:, columns(k)].astype(F32)) * weights
        grads[(k,) + mine] = grad.astype(BF16)
        share_grad(levels - 1, k)
        if mixing:
            send(
                ("yp", k),
                proj.at[(k,) + own],
                partner_proj.at[k],
                y_send.at[chunks + k],
                y_recv.at[chunks + k],
                other,
            )
        projected_ref[:, columns(k)] = summed.astype(BF16)

    def gather_stage(level, k):
        wait_recv("g", level, k)
        if level > 0:
            share_grad(level - 1, k)
            return
        if k == 0:
            loads[1].wait()
        block = flat(grads[k])
        weight = proj[(k,) + own]
        gradient = jnp.dot(attn_t[...], block, preferred_element_type=F32) * scaling
        moment = (BETA_MOM * mom[:, columns(k)].astype(F32) + gradient).astype(BF16)
        if mixing:
            moments[k] = moment
            send(
                ("y", k),
                moments.at[k],
                partner_moments.at[k],
                y_send.at[k],
                y_recv.at[k],
                other,
            )
        else:
            put(k, updated_of(weight, moment), moment)
        total[...] += lax.dot_general(
            block, weight, (((1,), (1,)), ((), ())), preferred_element_type=F32
        )

    def put(k, new_proj, new_moment):
        out_proj_ref[:, columns(k)] = new_proj
        out_mom_ref[:, columns(k)] = new_moment

    def updated_of(weight, moment):
        return (weight.astype(F32) - STEP_RATE * moment.astype(F32)).astype(BF16)

    def mix_stage(k):
        if not mixing:
            return
        copies["yp", k].wait_recv()
        copies["y", k].wait_recv()
        ours, theirs = moments[k], partner_moments[k]
        one = updated_of(proj[(k,) + own], ours).astype(F32)
        two = updated_of(partner_proj[k], theirs).astype(F32)
        put(
            k,
            ((one + two) * 0.5).astype(BF16),
            ((ours.astype(F32) + theirs.astype(F32)) * 0.5).astype(BF16),
        )

    len_group = len(group) + 1
    stages = [first]
    stages += [partial(proj_stage, level) for level in range(local - 1, 0, -1)]
    stages += [product]
    stages += [partial(reduce_stage, level) for level in range(local, levels)]
    stages += [partial(gather_stage, level) for level in range(levels - 1, -1, -1)]
    stages += [mix_stage]

    order = order_of(hops_of(radices, local, replicas, chunks, rows, depth, width), chunks)
    ahead = 0
    while ahead < len(order) and order[ahead][0] == 0:
        first(order[ahead][1])
        ahead += 1
    attn_group[own] = attn[outer_all + own]

    seg = seg_ref[...].astype(F32)
    shape = (rows, tokens)
    row_at = lax.broadcasted_iota(jnp.int32, shape, 0) + me * rows
    col_at = lax.broadcasted_iota(jnp.int32, shape, 1)
    seg_all = jnp.broadcast_to(seg, shape)
    own_seg = jnp.sum(jnp.where(row_at == col_at, seg_all, 0.0), axis=1, keepdims=True)
    count = jnp.sum(jnp.where(seg_all == own_seg, 1.0, 0.0), axis=1, keepdims=True)
    weights = tokens / (SEGS * count)
    attn_t[...] = flat(attn[...]).T
    total[...] = jnp.zeros_like(total)

    for j, k in order[ahead:]:
        stages[j](k)

    attn_grad_ref[...] = (total[...] * scaling).astype(BF16)
    for copy in copies.values():
        copy.wait_send()


def fused(attn, proj, mom, seg, target, radices, replicas, mixing):
    size, rows, wide = target.shape
    tokens, depth = size * rows, proj.shape[0]
    chunks = CHUNKS
    width = wide // chunks
    levels = len(radices)
    local = min(2, levels)
    most = max(radices) - 1
    scaling = (depth * size) ** (-0.5)
    dims = tuple(reversed(radices))
    sums, landed = [], []
    for level in range(local, levels):
        high = tuple(reversed(radices[level + 1 :]))
        sums.append(pltpu.VMEM((chunks,) + high + (radices[level], rows, width), BF16))
        landed.append(pltpu.VMEM((chunks, radices[level] - 1) + high + (rows, width), BF16))
    outer_dims, local_dims = dims[: levels - local], dims[levels - local :]
    group = 1
    for radix in local_dims:
        group *= radix
    vmem = pl.BlockSpec(memory_space=pltpu.VMEM)
    any_place = pl.BlockSpec(memory_space=pl.ANY)
    dma = pltpu.SemaphoreType.DMA
    return pl.pallas_call(
        functools.partial(kernel, radices, local, replicas, chunks, mixing, scaling),
        out_shape=(
            jax.ShapeDtypeStruct((rows, wide), BF16),
            jax.ShapeDtypeStruct((tokens, depth), BF16),
            jax.ShapeDtypeStruct((depth, wide), BF16),
            jax.ShapeDtypeStruct((depth, wide), BF16),
        ),
        in_specs=[
            any_place,
            any_place,
            any_place,
            vmem,
            any_place,
        ],
        out_specs=(vmem,) * 4,
        scratch_shapes=sums
        + landed
        + [
            pltpu.VMEM(dims + (rows, depth), BF16),
            pltpu.VMEM(local_dims + outer_dims + (rows, depth), BF16),
            pltpu.VMEM((chunks,) + local_dims + (depth, width), BF16),
            pltpu.VMEM((depth, wide), BF16),
            pltpu.VMEM((rows, wide), BF16),
            pltpu.VMEM((chunks,) + dims + (rows, width), BF16),
            pltpu.VMEM((chunks, depth, width), BF16),
            pltpu.VMEM((chunks, depth, width), BF16),
            pltpu.VMEM((chunks, depth, width), BF16),
            pltpu.VMEM((depth, tokens), BF16),
            pltpu.VMEM((tokens, depth), F32),
            dma((3,)),
            dma((chunks,)),
            dma((group,)),
            dma((group,)),
            dma((levels, chunks, most)),
            dma((levels, chunks, most)),
            dma((levels, chunks, most)),
            dma((levels, chunks, most)),
            dma((levels, chunks, most)),
            dma((levels, chunks, most)),
            dma((2 * chunks,)),
            dma((2 * chunks,)),
        ],
        cost_estimate=pl.CostEstimate(
            flops=6 * tokens * depth * wide, bytes_accessed=8 * depth * wide, transcendentals=0
        ),
        compiler_params=pltpu.CompilerParams(
            collective_id=0, has_side_effects=True, vmem_limit_bytes=VMEM_BYTES
        ),
    )(attn.reshape(dims + (rows, depth)), proj, mom, seg, target)


def passed_along(x, axis, by):
    size = lax.axis_size(axis)
    return lax.ppermute(x, axis, [(i, (i + by) % size) for i in range(size)])


def on_device(attn_out, proj, momentum, target, segment_ids, step):
    tensor_size = lax.axis_size("tensor")
    replicas = lax.axis_size("replica")
    rows_each = target.shape[1] // tensor_size
    bits = replicas.bit_length() - 1
    projected, attn_grad, updated, moment = fused(
        attn_out[0],
        proj[0],
        momentum[0],
        segment_ids,
        target[0].reshape(tensor_size, rows_each, target.shape[2]),
        radices_of(tensor_size),
        replicas,
        replicas == 2,
    )
    if replicas > 2:
        stacked = jnp.stack((updated, moment))
        branches = [
            partial(passed_along, axis="replica", by=1 << bit_pos) for bit_pos in range(bits)
        ]
        partner = lax.switch(step[0] % bits, branches, stacked)
        mixed = ((stacked.astype(F32) + partner.astype(F32)) * 0.5).astype(BF16)
        updated, moment = mixed[0], mixed[1]
    return (projected[None], attn_grad[None], updated[None], moment[None])


def solution(mesh):
    return jax.shard_map(
        on_device,
        mesh=mesh,
        in_specs=(
            P("replica", None, "tensor"),
            P("replica", "tensor", None),
            P("replica", "tensor", None),
            P("replica", None, None),
            P("replica", None),
            P(),
        ),
        out_specs=(
            P("replica", "tensor", None),
            P("replica", None, "tensor"),
            P("replica", "tensor", None),
            P("replica", "tensor", None),
        ),
        check_vma=False,
    )
```

```python
import functools
import itertools
from functools import partial

import jax
import jax.numpy as jnp
from jax import lax
from jax.experimental import pallas as pl
from jax.experimental.pallas import tpu as pltpu
from jax.sharding import PartitionSpec as P

SEGS = 96
BETA_MOM = 0.9
STEP_RATE = 0.1
CHUNKS = 16
HOP_US = 1.5
AHEAD = 5
LINK_GB = 100.0
VMEM_BYTES = 52 * 1024 * 1024
BF16 = jnp.bfloat16
F32 = jnp.float32
MESH = pl.DeviceIdType.MESH


def radices_of(size):
    found = []
    while size > 2 and size % 2 == 0:
        found.append(2)
        size //= 2
    if size > 1:
        found.append(size)
    return tuple(found)


def hops_of(radices, local, replicas, chunks, rows, depth, width):
    levels = len(radices)
    block = 2e-6 * rows * width / LINK_GB
    weight = 2e-6 * depth * width / LINK_GB
    hops = []

    def add(level, time, work):
        chip = level > 0
        hops.append((level, 1e3 * time * (2 if chip else 1 / 6), work))

    for level in range(local - 1, -1, -1):
        held = 1
        for radix in radices[level + 1 : local]:
            held *= radix
        add(level, weight * held, 0.2)
    size = 1
    for radix in radices[local:]:
        size *= radix
    for level in range(local, levels):
        size //= radices[level]
        far = min(2, level - local + 1)
        add(level if level == local else local, block * size * far, 0.3)
    held = 1
    for level in range(levels - 1, -1, -1):
        far = 2 if level > local else 1
        add(min(level, local), block * held * far, 0.3)
        held *= radices[level]
    hops.append(("y", 2e3 * weight, 0.6))
    return hops


def order_of(hops, chunks):
    free, now, order = {}, 0.0, []
    ready = {(0, k): 0.0 for k in range(min(AHEAD, chunks))}
    while ready:
        task = min(ready, key=lambda at: (max(ready[at], now), -at[0] if at[0] else 1, at[1]))
        stage, k = task
        now = max(now, ready.pop(task))
        order.append(task)
        if stage == 1 and k + AHEAD < chunks:
            ready[0, k + AHEAD] = now
        if stage < len(hops):
            link, time, work = hops[stage]
            now += work
            begin = max(now, free.get(link, 0.0))
            free[link] = begin + time
            ready[stage + 1, k] = begin + time + HOP_US
        else:
            now += 0.3
    return order


def kernel(
    radices,
    local,
    replicas,
    chunks,
    mixing,
    scaling,
    attn_hbm,
    proj_hbm,
    mom_hbm,
    seg_ref,
    target_hbm,
    projected_ref,
    attn_grad_ref,
    out_proj_ref,
    out_mom_ref,
    *scratch,
):
    levels = len(radices)
    outer = levels - local
    sums = scratch[:outer]
    landed = scratch[outer : 2 * outer]
    (
        attn,
        attn_group,
        proj,
        mom,
        target,
        grads,
        moments,
        partner_moments,
        partner_proj,
        attn_t,
        total,
        in_sem,
        proj_sem,
        a_send,
        a_recv,
        p_send,
        p_recv,
        rs_send,
        rs_recv,
        ag_send,
        ag_recv,
        y_send,
        y_recv,
    ) = scratch[2 * outer :]
    rows, depth = attn.shape[-2:]
    width = proj.shape[-1]
    me = lax.axis_index("tensor")
    rep = lax.axis_index("replica")
    digits, strides, rest, stride = [], [], me, 1
    for radix in radices:
        digits.append(lax.rem(rest, radix))
        strides.append(stride)
        rest = lax.div(rest, radix)
        stride *= radix
    tokens = stride * rows
    mine = tuple(reversed(digits))
    own = tuple(reversed(digits[:local]))
    outer_all = (slice(None),) * outer

    def peer(level, by):
        to = lax.rem(digits[level] + by, radices[level])
        return to, me + (to - digits[level]) * strides[level]

    group = []
    for offsets in itertools.product(*[range(r) for r in reversed(radices[:local])]):
        if any(offsets):
            there, index = [], me
            for level, by in zip(range(local - 1, -1, -1), offsets):
                to, _ = peer(level, by)
                there.append(to)
                index = index + (to - digits[level]) * strides[level]
            group.append((tuple(there), index))

    other = {"replica": lax.rem(rep + 1, replicas)}

    def columns(k):
        return slice(k * width, (k + 1) * width)

    loads = [
        pltpu.make_async_copy(attn_hbm, attn, in_sem.at[0]),
        pltpu.make_async_copy(mom_hbm, mom, in_sem.at[1]),
        pltpu.make_async_copy(target_hbm.at[me], target, in_sem.at[2]),
    ]
    proj_loads = [
        pltpu.make_async_copy(proj_hbm.at[:, columns(k)], proj.at[(k,) + own], proj_sem.at[k])
        for k in range(chunks)
    ]
    loads[0].start()
    for load in proj_loads:
        load.start()
    loads[1].start()
    loads[2].start()

    barrier = pltpu.get_barrier_semaphore()
    greet = [{"tensor": index} for _, index in group]
    for level in range(local, levels):
        greet += [{"tensor": peer(level, by)[1]} for by in range(1, radices[level])]
    if mixing:
        greet.append(other)
    for device in greet:
        pl.semaphore_signal(barrier, inc=1, device_id=device, device_id_type=MESH)
    loads[0].wait()
    pl.semaphore_wait(barrier, len(greet))

    copies = {}

    def send(key, src, dst, send_sem, recv_sem, device):
        copy = pltpu.make_async_remote_copy(
            src_ref=src,
            dst_ref=dst,
            send_sem=send_sem,
            recv_sem=recv_sem,
            device_id=device,
            device_id_type=MESH,
        )
        copy.start()
        copies[key] = copy

    for i, (there, index) in enumerate(group):
        send(
            ("a", i),
            attn.at[outer_all + there],
            attn_group.at[own],
            a_send.at[i],
            a_recv.at[i],
            {"tensor": index},
        )

    def gather(kind, ref, sems, level, k, high):
        place = (k,) + high + tuple(digits[i] for i in range(level, -1, -1))
        for by in range(1, radices[level]):
            send(
                (kind, level, k, by),
                ref.at[place],
                ref.at[place],
                sems[0].at[level, k, by - 1],
                sems[1].at[level, k, by - 1],
                {"tensor": peer(level, by)[1]},
            )

    def share_proj(level, k):
        gather("p", proj, (p_send, p_recv), level, k, (slice(None),) * (local - 1 - level))

    def share_grad(level, k):
        gather("g", grads, (ag_send, ag_recv), level, k, (slice(None),) * (levels - 1 - level))

    def reduce_start(level, k):
        high = (slice(None),) * (levels - 1 - level)
        for by in range(1, radices[level]):
            to, index = peer(level, by)
            send(
                ("r", level, k, by),
                sums[level - local].at[(k,) + high + (to,)],
                landed[level - local].at[k, by - 1],
                rs_send.at[level, k, by - 1],
                rs_recv.at[level, k, by - 1],
                {"tensor": index},
            )

    def wait_recv(kind, level, k):
        for by in range(1, radices[level]):
            copies[kind, level, k, by].wait_recv()

    def first(k):
        proj_loads[k].wait()
        if local > 0:
            share_proj(local - 1, k)

    def proj_stage(level, k):
        wait_recv("p", level, k)
        share_proj(level - 1, k)

    def product(k):
        if local > 0:
            wait_recv("p", 0, k)
        if k == 0:
            for i in range(len(group)):
                copies["a", i].wait_recv()
        part = jnp.zeros((tokens // len_group, width), F32)
        for at in itertools.product(*[range(r) for r in reversed(radices[:local])]):
            left = attn_group[at]
            part = part + jnp.dot(flat(left), proj[(k,) + at], preferred_element_type=F32)
        shape = tuple(reversed(radices[local:])) + (rows, width)
        part = part.reshape(shape)
        if outer > 0:
            sums[0][k] = part.astype(BF16)
            reduce_start(local, k)
        else:
            finish(part, k)

    def flat(block):
        count = 1
        for n in block.shape[:-1]:
            count *= n
        if rows % 16:
            return block.astype(F32).reshape(count, block.shape[-1]).astype(BF16)
        return block.reshape(count, block.shape[-1])

    def reduce_stage(level, k):
        wait_recv("r", level, k)
        high = (slice(None),) * (levels - 1 - level)
        value = sums[level - local][(k,) + high + (digits[level],)].astype(F32)
        for by in range(1, radices[level]):
            value = value + landed[level - local][k, by - 1].astype(F32)
        if level + 1 < levels:
            sums[level + 1 - local][k] = value.astype(BF16)
            reduce_start(level + 1, k)
        else:
            finish(value, k)

    def finish(value, k):
        if k == 0:
            loads[2].wait()
        summed = value * scaling
        grad = (summed - target[:, columns(k)].astype(F32)) * weights
        grads[(k,) + mine] = grad.astype(BF16)
        share_grad(levels - 1, k)
        if mixing:
            send(
                ("yp", k),
                proj.at[(k,) + own],
                partner_proj.at[k],
                y_send.at[chunks + k],
                y_recv.at[chunks + k],
                other,
            )
        projected_ref[:, columns(k)] = summed.astype(BF16)

    def gather_stage(level, k):
        wait_recv("g", level, k)
        if level > 0:
            share_grad(level - 1, k)
            return
        if k == 0:
            loads[1].wait()
        block = flat(grads[k])
        weight = proj[(k,) + own]
        gradient = jnp.dot(attn_t[...], block, preferred_element_type=F32) * scaling
        moment = (BETA_MOM * mom[:, columns(k)].astype(F32) + gradient).astype(BF16)
        if mixing:
            moments[k] = moment
            send(
                ("y", k),
                moments.at[k],
                partner_moments.at[k],
                y_send.at[k],
                y_recv.at[k],
                other,
            )
        else:
            put(k, updated_of(weight, moment), moment)
        total[...] += lax.dot_general(
            block, weight, (((1,), (1,)), ((), ())), preferred_element_type=F32
        )

    def put(k, new_proj, new_moment):
        out_proj_ref[:, columns(k)] = new_proj
        out_mom_ref[:, columns(k)] = new_moment

    def updated_of(weight, moment):
        return (weight.astype(F32) - STEP_RATE * moment.astype(F32)).astype(BF16)

    def mix_stage(k):
        if not mixing:
            return
        copies["yp", k].wait_recv()
        copies["y", k].wait_recv()
        ours, theirs = moments[k], partner_moments[k]
        one = updated_of(proj[(k,) + own], ours).astype(F32)
        two = updated_of(partner_proj[k], theirs).astype(F32)
        put(
            k,
            ((one + two) * 0.5).astype(BF16),
            ((ours.astype(F32) + theirs.astype(F32)) * 0.5).astype(BF16),
        )

    len_group = len(group) + 1
    stages = [first]
    stages += [partial(proj_stage, level) for level in range(local - 1, 0, -1)]
    stages += [product]
    stages += [partial(reduce_stage, level) for level in range(local, levels)]
    stages += [partial(gather_stage, level) for level in range(levels - 1, -1, -1)]
    stages += [mix_stage]

    order = order_of(hops_of(radices, local, replicas, chunks, rows, depth, width), chunks)
    ahead = 0
    while ahead < len(order) and order[ahead][0] == 0:
        first(order[ahead][1])
        ahead += 1
    attn_group[own] = attn[outer_all + own]

    seg = seg_ref[...].astype(F32)
    shape = (rows, tokens)
    row_at = lax.broadcasted_iota(jnp.int32, shape, 0) + me * rows
    col_at = lax.broadcasted_iota(jnp.int32, shape, 1)
    seg_all = jnp.broadcast_to(seg, shape)
    own_seg = jnp.sum(jnp.where(row_at == col_at, seg_all, 0.0), axis=1, keepdims=True)
    count = jnp.sum(jnp.where(seg_all == own_seg, 1.0, 0.0), axis=1, keepdims=True)
    weights = tokens / (SEGS * count)
    attn_t[...] = flat(attn[...]).T
    total[...] = jnp.zeros_like(total)

    for j, k in order[ahead:]:
        stages[j](k)

    attn_grad_ref[...] = (total[...] * scaling).astype(BF16)
    for copy in copies.values():
        copy.wait_send()


def fused(attn, proj, mom, seg, target, radices, replicas, mixing):
    size, rows, wide = target.shape
    tokens, depth = size * rows, proj.shape[0]
    chunks = CHUNKS
    width = wide // chunks
    levels = len(radices)
    local = min(2, levels)
    most = max(radices) - 1
    scaling = (depth * size) ** (-0.5)
    dims = tuple(reversed(radices))
    sums, landed = [], []
    for level in range(local, levels):
        high = tuple(reversed(radices[level + 1 :]))
        sums.append(pltpu.VMEM((chunks,) + high + (radices[level], rows, width), BF16))
        landed.append(pltpu.VMEM((chunks, radices[level] - 1) + high + (rows, width), BF16))
    outer_dims, local_dims = dims[: levels - local], dims[levels - local :]
    group = 1
    for radix in local_dims:
        group *= radix
    vmem = pl.BlockSpec(memory_space=pltpu.VMEM)
    any_place = pl.BlockSpec(memory_space=pl.ANY)
    dma = pltpu.SemaphoreType.DMA
    return pl.pallas_call(
        functools.partial(kernel, radices, local, replicas, chunks, mixing, scaling),
        out_shape=(
            jax.ShapeDtypeStruct((rows, wide), BF16),
            jax.ShapeDtypeStruct((tokens, depth), BF16),
            jax.ShapeDtypeStruct((depth, wide), BF16),
            jax.ShapeDtypeStruct((depth, wide), BF16),
        ),
        in_specs=[
            any_place,
            any_place,
            any_place,
            vmem,
            any_place,
        ],
        out_specs=(vmem,) * 4,
        scratch_shapes=sums
        + landed
        + [
            pltpu.VMEM(dims + (rows, depth), BF16),
            pltpu.VMEM(local_dims + outer_dims + (rows, depth), BF16),
            pltpu.VMEM((chunks,) + local_dims + (depth, width), BF16),
            pltpu.VMEM((depth, wide), BF16),
            pltpu.VMEM((rows, wide), BF16),
            pltpu.VMEM((chunks,) + dims + (rows, width), BF16),
            pltpu.VMEM((chunks, depth, width), BF16),
            pltpu.VMEM((chunks, depth, width), BF16),
            pltpu.VMEM((chunks, depth, width), BF16),
            pltpu.VMEM((depth, tokens), BF16),
            pltpu.VMEM((tokens, depth), F32),
            dma((3,)),
            dma((chunks,)),
            dma((group,)),
            dma((group,)),
            dma((levels, chunks, most)),
            dma((levels, chunks, most)),
            dma((levels, chunks, most)),
            dma((levels, chunks, most)),
            dma((levels, chunks, most)),
            dma((levels, chunks, most)),
            dma((2 * chunks,)),
            dma((2 * chunks,)),
        ],
        cost_estimate=pl.CostEstimate(
            flops=6 * tokens * depth * wide, bytes_accessed=8 * depth * wide, transcendentals=0
        ),
        compiler_params=pltpu.CompilerParams(
            collective_id=0, has_side_effects=True, vmem_limit_bytes=VMEM_BYTES
        ),
    )(attn.reshape(dims + (rows, depth)), proj, mom, seg, target)


def passed_along(x, axis, by):
    size = lax.axis_size(axis)
    return lax.ppermute(x, axis, [(i, (i + by) % size) for i in range(size)])


def on_device(attn_out, proj, momentum, target, segment_ids, step):
    tensor_size = lax.axis_size("tensor")
    replicas = lax.axis_size("replica")
    rows_each = target.shape[1] // tensor_size
    bits = replicas.bit_length() - 1
    projected, attn_grad, updated, moment = fused(
        attn_out[0],
        proj[0],
        momentum[0],
        segment_ids,
        target[0].reshape(tensor_size, rows_each, target.shape[2]),
        radices_of(tensor_size),
        replicas,
        replicas == 2,
    )
    if replicas > 2:
        stacked = jnp.stack((updated, moment))
        branches = [
            partial(passed_along, axis="replica", by=1 << bit_pos) for bit_pos in range(bits)
        ]
        partner = lax.switch(step[0] % bits, branches, stacked)
        mixed = ((stacked.astype(F32) + partner.astype(F32)) * 0.5).astype(BF16)
        updated, moment = mixed[0], mixed[1]
    return (projected[None], attn_grad[None], updated[None], moment[None])


def solution(mesh):
    return jax.shard_map(
        on_device,
        mesh=mesh,
        in_specs=(
            P("replica", None, "tensor"),
            P("replica", "tensor", None),
            P("replica", "tensor", None),
            P("replica", None, None),
            P("replica", None),
            P(),
        ),
        out_specs=(
            P("replica", "tensor", None),
            P("replica", None, "tensor"),
            P("replica", "tensor", None),
            P("replica", "tensor", None),
        ),
        check_vma=False,
    )
```

```python
import functools
import itertools
from functools import partial

import jax
import jax.numpy as jnp
from jax import lax
from jax.experimental import pallas as pl
from jax.experimental.pallas import tpu as pltpu
from jax.sharding import PartitionSpec as P

SEGS = 96
BETA_MOM = 0.9
STEP_RATE = 0.1
SHARES = (1, 1, 1, 1, 1, 1, 1, 1)
HOP_US = 1.5
AHEAD = 3
LINK_GB = 100.0
VMEM_BYTES = 52 * 1024 * 1024
BF16 = jnp.bfloat16
F32 = jnp.float32
MESH = pl.DeviceIdType.MESH


def radices_of(size):
    found = []
    while size > 2 and size % 2 == 0:
        found.append(2)
        size //= 2
    if size > 1:
        found.append(size)
    return tuple(found)


def hops_of(radices, local, rows, depth, width):
    levels = len(radices)
    block = 2e-6 * rows * width / LINK_GB
    weight = 2e-6 * depth * width / LINK_GB
    hops = []

    def add(level, time, work):
        chip = level > 0
        hops.append((level, 1e3 * time * (2 if chip else 1 / 6), work))

    for level in range(local - 1, -1, -1):
        held = 1
        for radix in radices[level + 1 : local]:
            held *= radix
        add(level, weight * held, 0.2)
    size = 1
    for radix in radices[local:]:
        size *= radix
    for level in range(local, levels):
        size //= radices[level]
        far = min(2, level - local + 1)
        add(level if level == local else local, block * size * far, 0.3)
    held = 1
    for level in range(levels - 1, -1, -1):
        far = 2 if level > local else 1
        add(min(level, local), block * held * far, 0.3)
        held *= radices[level]
    hops.append(("y", 2e3 * weight, 0.6))
    return hops


def order_of(hops, shares):
    free, now, order, chunks = {}, 0.0, [], len(shares)
    ready = {(0, k): 0.0 for k in range(min(AHEAD, chunks))}
    while ready:
        task = min(ready, key=lambda at: (max(ready[at], now), -at[0] if at[0] else 1, at[1]))
        stage, k = task
        now = max(now, ready.pop(task))
        order.append(task)
        if stage == 1 and k + AHEAD < chunks:
            ready[0, k + AHEAD] = now
        if stage < len(hops):
            link, time, work = hops[stage]
            now += work
            time = time * shares[k]
            begin = max(now, free.get(link, 0.0))
            free[link] = begin + time
            ready[stage + 1, k] = begin + time + HOP_US
        else:
            now += 0.3
    return order


def kernel(
    radices,
    local,
    replicas,
    widths,
    mixing,
    scaling,
    attn_hbm,
    proj_hbm,
    mom_hbm,
    seg_ref,
    target_hbm,
    projected_ref,
    attn_grad_ref,
    out_proj_ref,
    out_mom_ref,
    *scratch,
):
    levels = len(radices)
    outer = levels - local
    (
        sums,
        landed,
        attn_raw,
        attn,
        attn_group,
        proj,
        mom,
        target,
        grads,
        moments,
        partner_moments,
        partner_proj,
        attn_t,
        total,
        in_sem,
        proj_sem,
        a_send,
        a_recv,
        p_send,
        p_recv,
        rs_send,
        rs_recv,
        ag_send,
        ag_recv,
        y_send,
        y_recv,
    ) = scratch
    rows, depth = attn.shape[-2:]
    chunks = len(widths)
    me = lax.axis_index("tensor")
    rep = lax.axis_index("replica")
    digits, strides, rest, stride = [], [], me, 1
    for radix in radices:
        digits.append(lax.rem(rest, radix))
        strides.append(stride)
        rest = lax.div(rest, radix)
        stride *= radix
    tokens = stride * rows
    mine = tuple(digits)
    own = tuple(digits[:local])
    blocks = list(itertools.product(*[range(radix) for radix in radices]))

    def peer(level, by):
        to = lax.rem(digits[level] + by, radices[level])
        return to, me + (to - digits[level]) * strides[level]

    group = []
    for offsets in itertools.product(*[range(r) for r in radices[:local]]):
        if any(offsets):
            there, index = [], me
            for level, by in zip(range(local), offsets):
                to, _ = peer(level, by)
                there.append(to)
                index = index + (to - digits[level]) * strides[level]
            group.append((tuple(there), index))

    other = {"replica": lax.rem(rep + 1, replicas)}

    def columns(k):
        return slice(sum(widths[:k]), sum(widths[: k + 1]))

    loads = [
        pltpu.make_async_copy(attn_hbm, attn_raw, in_sem.at[0]),
        pltpu.make_async_copy(mom_hbm, mom, in_sem.at[1]),
        pltpu.make_async_copy(target_hbm.at[me], target, in_sem.at[2]),
    ]
    proj_loads = [
        pltpu.make_async_copy(proj_hbm.at[:, columns(k)], proj[k].at[own], proj_sem.at[k])
        for k in range(chunks)
    ]
    loads[0].start()
    for load in proj_loads:
        load.start()
    loads[1].start()
    loads[2].start()

    barrier = pltpu.get_barrier_semaphore()
    greet = [{"tensor": index} for _, index in group]
    for level in range(local, levels):
        greet += [{"tensor": peer(level, by)[1]} for by in range(1, radices[level])]
    if mixing:
        greet.append(other)
    for device in greet:
        pl.semaphore_signal(barrier, inc=1, device_id=device, device_id_type=MESH)
    loads[0].wait()
    for at in blocks:
        attn[at] = attn_raw[tuple(reversed(at))]
    pl.semaphore_wait(barrier, len(greet))

    copies = {}

    def send(key, src, dst, send_sem, recv_sem, device):
        copy = pltpu.make_async_remote_copy(
            src_ref=src,
            dst_ref=dst,
            send_sem=send_sem,
            recv_sem=recv_sem,
            device_id=device,
            device_id_type=MESH,
        )
        copy.start()
        copies[key] = copy

    for i, (there, index) in enumerate(group):
        send(
            ("a", i),
            attn.at[there],
            attn_group.at[own],
            a_send.at[i],
            a_recv.at[i],
            {"tensor": index},
        )

    def gather(kind, ref, sems, level, k):
        place = tuple(digits[: level + 1])
        for by in range(1, radices[level]):
            send(
                (kind, level, k, by),
                ref[k].at[place],
                ref[k].at[place],
                sems[0].at[level, k, by - 1],
                sems[1].at[level, k, by - 1],
                {"tensor": peer(level, by)[1]},
            )

    def share_proj(level, k):
        gather("p", proj, (p_send, p_recv), level, k)

    def share_grad(level, k):
        gather("g", grads, (ag_send, ag_recv), level, k)

    def reduce_start(level, k):
        for by in range(1, radices[level]):
            to, index = peer(level, by)
            send(
                ("r", level, k, by),
                sums[level - local][k].at[to],
                landed[level - local][k].at[by - 1],
                rs_send.at[level, k, by - 1],
                rs_recv.at[level, k, by - 1],
                {"tensor": index},
            )

    def wait_recv(kind, level, k):
        for by in range(1, radices[level]):
            copies[kind, level, k, by].wait_recv()

    def first(k):
        proj_loads[k].wait()
        if local > 0:
            share_proj(local - 1, k)

    def proj_stage(level, k):
        wait_recv("p", level, k)
        share_proj(level - 1, k)

    def product(k):
        if local > 0:
            wait_recv("p", 0, k)
        if k == 0:
            for i in range(len(group)):
                copies["a", i].wait_recv()
        part = jnp.zeros((tokens // len_group, widths[k]), F32)
        for at in itertools.product(*[range(r) for r in radices[:local]]):
            left = attn_group[at]
            part = part + jnp.dot(flat(left), proj[k][at], preferred_element_type=F32)
        shape = tuple(radices[local:]) + (rows, widths[k])
        part = part.reshape(shape)
        if outer > 0:
            sums[0][k][...] = part.astype(BF16)
            reduce_start(local, k)
        else:
            finish(part, k)

    def flat(block):
        count = 1
        for n in block.shape[:-1]:
            count *= n
        if rows % 16:
            return block.astype(F32).reshape(count, block.shape[-1]).astype(BF16)
        return block.reshape(count, block.shape[-1])

    def reduce_stage(level, k):
        wait_recv("r", level, k)
        value = sums[level - local][k][digits[level]].astype(F32)
        for by in range(1, radices[level]):
            value = value + landed[level - local][k][by - 1].astype(F32)
        if level + 1 < levels:
            sums[level + 1 - local][k][...] = value.astype(BF16)
            reduce_start(level + 1, k)
        else:
            finish(value, k)

    def finish(value, k):
        if k == 0:
            loads[2].wait()
        summed = value * scaling
        grad = (summed - target[:, columns(k)].astype(F32)) * weights
        grads[k][mine] = grad.astype(BF16)
        share_grad(levels - 1, k)
        projected_ref[:, columns(k)] = summed.astype(BF16)

    def gather_stage(level, k):
        wait_recv("g", level, k)
        if level > 0:
            share_grad(level - 1, k)
            return
        if k == 0:
            loads[1].wait()
        block = flat(grads[k][...])
        weight = proj[k][own]
        gradient = jnp.dot(attn_t[...], block, preferred_element_type=F32) * scaling
        moment = (BETA_MOM * mom[:, columns(k)].astype(F32) + gradient).astype(BF16)
        if mixing:
            moments[k][...] = moment
            send(
                ("y", k),
                moments[k],
                partner_moments[k],
                y_send.at[k],
                y_recv.at[k],
                other,
            )
        else:
            put(k, updated_of(weight, moment), moment)
        total[...] += lax.dot_general(
            block, weight, (((1,), (1,)), ((), ())), preferred_element_type=F32
        )

    def put(k, new_proj, new_moment):
        out_proj_ref[:, columns(k)] = new_proj
        out_mom_ref[:, columns(k)] = new_moment

    def updated_of(weight, moment):
        return (weight.astype(F32) - STEP_RATE * moment.astype(F32)).astype(BF16)

    def mix_stage(k):
        if not mixing:
            return
        if k == 0:
            copies["yp"].wait_recv()
        copies["y", k].wait_recv()
        ours, theirs = moments[k][...], partner_moments[k][...]
        one = updated_of(proj[k][own], ours).astype(F32)
        two = updated_of(partner_proj[:, columns(k)], theirs).astype(F32)
        put(
            k,
            ((one + two) * 0.5).astype(BF16),
            ((ours.astype(F32) + theirs.astype(F32)) * 0.5).astype(BF16),
        )

    len_group = len(group) + 1
    stages = [first]
    stages += [partial(proj_stage, level) for level in range(local - 1, 0, -1)]
    stages += [product]
    stages += [partial(reduce_stage, level) for level in range(local, levels)]
    stages += [partial(gather_stage, level) for level in range(levels - 1, -1, -1)]
    stages += [mix_stage]

    shares = tuple(width / widths[0] for width in widths)
    order = order_of(hops_of(radices, local, rows, depth, widths[0]), shares)
    ahead = 0
    while ahead < len(order) and order[ahead][0] == 0:
        first(order[ahead][1])
        ahead += 1
    if mixing:
        send("yp", proj_hbm, partner_proj, y_send.at[chunks], y_recv.at[chunks], other)
    attn_group[own] = attn[own]

    seg = seg_ref[...].astype(F32)
    shape = (rows, tokens)
    row_at = lax.broadcasted_iota(jnp.int32, shape, 0) + me * rows
    col_at = lax.broadcasted_iota(jnp.int32, shape, 1)
    seg_all = jnp.broadcast_to(seg, shape)
    own_seg = jnp.sum(jnp.where(row_at == col_at, seg_all, 0.0), axis=1, keepdims=True)
    count = jnp.sum(jnp.where(seg_all == own_seg, 1.0, 0.0), axis=1, keepdims=True)
    weights = tokens / (SEGS * count)
    attn_t[...] = flat(attn[...]).T
    total[...] = jnp.zeros_like(total)

    for j, k in order[ahead:]:
        stages[j](k)

    for i, at in enumerate(blocks):
        place = sum(digit * stride for digit, stride in zip(at, strides))
        attn_grad_ref[place] = (total[i * rows : (i + 1) * rows, :] * scaling).astype(BF16)
    for copy in copies.values():
        copy.wait_send()


def per_chunk(widths, shape):
    return [pltpu.VMEM(tuple(shape) + (width,), BF16) for width in widths]


def fused(attn, proj, mom, seg, target, radices, replicas, mixing):
    size, rows, wide = target.shape
    tokens, depth = size * rows, proj.shape[0]
    widths = tuple(wide // sum(SHARES) * share for share in SHARES)
    chunks = len(widths)
    levels = len(radices)
    local = min(2, levels)
    most = max(radices) - 1
    scaling = (depth * size) ** (-0.5)
    dims = tuple(radices)
    sums, landed = [], []
    for level in range(local, levels):
        high = dims[level + 1 :]
        sums.append(per_chunk(widths, (radices[level],) + high + (rows,)))
        landed.append(per_chunk(widths, (radices[level] - 1,) + high + (rows,)))
    local_dims, outer_dims = dims[:local], dims[local:]
    group = 1
    for radix in local_dims:
        group *= radix
    vmem = pl.BlockSpec(memory_space=pltpu.VMEM)
    any_place = pl.BlockSpec(memory_space=pl.ANY)
    dma = pltpu.SemaphoreType.DMA
    return pl.pallas_call(
        functools.partial(kernel, radices, local, replicas, widths, mixing, scaling),
        out_shape=(
            jax.ShapeDtypeStruct((rows, wide), BF16),
            jax.ShapeDtypeStruct((size, rows, depth), BF16),
            jax.ShapeDtypeStruct((depth, wide), BF16),
            jax.ShapeDtypeStruct((depth, wide), BF16),
        ),
        in_specs=[
            any_place,
            any_place,
            any_place,
            vmem,
            any_place,
        ],
        out_specs=(vmem,) * 4,
        scratch_shapes=[
            sums,
            landed,
            pltpu.VMEM(tuple(reversed(dims)) + (rows, depth), BF16),
            pltpu.VMEM(dims + (rows, depth), BF16),
            pltpu.VMEM(local_dims + outer_dims + (rows, depth), BF16),
            per_chunk(widths, local_dims + (depth,)),
            pltpu.VMEM((depth, wide), BF16),
            pltpu.VMEM((rows, wide), BF16),
            per_chunk(widths, dims + (rows,)),
            per_chunk(widths, (depth,)),
            per_chunk(widths, (depth,)),
            pltpu.VMEM((depth, wide), BF16),
            pltpu.VMEM((depth, tokens), BF16),
            pltpu.VMEM((tokens, depth), F32),
            dma((3,)),
            dma((chunks,)),
            dma((group,)),
            dma((group,)),
            dma((levels, chunks, most)),
            dma((levels, chunks, most)),
            dma((levels, chunks, most)),
            dma((levels, chunks, most)),
            dma((levels, chunks, most)),
            dma((levels, chunks, most)),
            dma((chunks + 1,)),
            dma((chunks + 1,)),
        ],
        cost_estimate=pl.CostEstimate(
            flops=6 * tokens * depth * wide, bytes_accessed=8 * depth * wide, transcendentals=0
        ),
        compiler_params=pltpu.CompilerParams(
            collective_id=0, has_side_effects=True, vmem_limit_bytes=VMEM_BYTES
        ),
    )(attn.reshape(tuple(reversed(dims)) + (rows, depth)), proj, mom, seg, target)


def passed_along(x, axis, by):
    size = lax.axis_size(axis)
    return lax.ppermute(x, axis, [(i, (i + by) % size) for i in range(size)])


def on_device(attn_out, proj, momentum, target, segment_ids, step):
    tensor_size = lax.axis_size("tensor")
    replicas = lax.axis_size("replica")
    rows_each = target.shape[1] // tensor_size
    bits = replicas.bit_length() - 1
    projected, attn_grad, updated, moment = fused(
        attn_out[0],
        proj[0],
        momentum[0],
        segment_ids,
        target[0].reshape(tensor_size, rows_each, target.shape[2]),
        radices_of(tensor_size),
        replicas,
        replicas == 2,
    )
    if replicas > 2:
        stacked = jnp.stack((updated, moment))
        branches = [
            partial(passed_along, axis="replica", by=1 << bit_pos) for bit_pos in range(bits)
        ]
        partner = lax.switch(step[0] % bits, branches, stacked)
        mixed = ((stacked.astype(F32) + partner.astype(F32)) * 0.5).astype(BF16)
        updated, moment = mixed[0], mixed[1]
    attn_grad = attn_grad.reshape(attn_out.shape)
    return (projected[None], attn_grad, updated[None], moment[None])


def solution(mesh):
    return jax.shard_map(
        on_device,
        mesh=mesh,
        in_specs=(
            P("replica", None, "tensor"),
            P("replica", "tensor", None),
            P("replica", "tensor", None),
            P("replica", None, None),
            P("replica", None),
            P(),
        ),
        out_specs=(
            P("replica", "tensor", None),
            P("replica", None, "tensor"),
            P("replica", "tensor", None),
            P("replica", "tensor", None),
        ),
        check_vma=False,
    )
```

```python
import functools
import itertools
from functools import partial

import jax
import jax.numpy as jnp
from jax import lax
from jax.experimental import pallas as pl
from jax.experimental.pallas import tpu as pltpu
from jax.sharding import PartitionSpec as P

SEGS = 96
BETA_MOM = 0.9
STEP_RATE = 0.1
SHARES = (1, 2, 2, 2, 1)
HOP_US = 1.5
AHEAD = 2
LINK_GB = 100.0
VMEM_BYTES = 52 * 1024 * 1024
BF16 = jnp.bfloat16
F32 = jnp.float32
MESH = pl.DeviceIdType.MESH


def radices_of(size):
    found = []
    while size > 2 and size % 2 == 0:
        found.append(2)
        size //= 2
    if size > 1:
        found.append(size)
    return tuple(found)


def hops_of(radices, local, rows, depth, width):
    levels = len(radices)
    block = 2e-6 * rows * width / LINK_GB
    weight = 2e-6 * depth * width / LINK_GB
    hops = []

    def add(level, time, work):
        chip = level > 0
        hops.append((level, 1e3 * time * (2 if chip else 1 / 6), work))

    for level in range(local - 1, -1, -1):
        held = 1
        for radix in radices[level + 1 : local]:
            held *= radix
        add(level, weight * held, 0.2)
    size = 1
    for radix in radices[local:]:
        size *= radix
    for level in range(local, levels):
        size //= radices[level]
        far = min(2, level - local + 1)
        add(level if level == local else local, block * size * far, 0.3)
    held = 1
    for level in range(levels - 1, -1, -1):
        far = 2 if level > local else 1
        add(min(level, local), block * held * far, 0.3)
        held *= radices[level]
    hops.append(("y", 2e3 * weight, 0.6))
    return hops


def order_of(hops, shares):
    free, now, order, chunks = {}, 0.0, [], len(shares)
    ready = {(0, k): 0.0 for k in range(min(AHEAD, chunks))}
    while ready:
        task = min(ready, key=lambda at: (max(ready[at], now), -at[0] if at[0] else 1, at[1]))
        stage, k = task
        now = max(now, ready.pop(task))
        order.append(task)
        if stage == 1 and k + AHEAD < chunks:
            ready[0, k + AHEAD] = now
        if stage < len(hops):
            link, time, work = hops[stage]
            now += work
            time = time * shares[k]
            begin = max(now, free.get(link, 0.0))
            free[link] = begin + time
            ready[stage + 1, k] = begin + time + HOP_US
        else:
            now += 0.3
    return order


def kernel(
    radices,
    local,
    replicas,
    widths,
    mixing,
    scaling,
    attn_hbm,
    proj_hbm,
    mom_hbm,
    seg_ref,
    target_hbm,
    projected_ref,
    attn_grad_ref,
    out_proj_ref,
    out_mom_ref,
    *scratch,
):
    levels = len(radices)
    outer = levels - local
    (
        sums,
        landed,
        attn_raw,
        attn,
        attn_group,
        proj,
        mom,
        target,
        grads,
        moments,
        partner_moments,
        partner_proj,
        attn_t,
        total,
        in_sem,
        proj_sem,
        a_send,
        a_recv,
        p_send,
        p_recv,
        rs_send,
        rs_recv,
        ag_send,
        ag_recv,
        y_send,
        y_recv,
    ) = scratch
    rows, depth = attn.shape[-2:]
    chunks = len(widths)
    me = lax.axis_index("tensor")
    rep = lax.axis_index("replica")
    digits, strides, rest, stride = [], [], me, 1
    for radix in radices:
        digits.append(lax.rem(rest, radix))
        strides.append(stride)
        rest = lax.div(rest, radix)
        stride *= radix
    tokens = stride * rows
    mine = tuple(digits)
    own = tuple(digits[:local])
    blocks = list(itertools.product(*[range(radix) for radix in radices]))

    def peer(level, by):
        to = lax.rem(digits[level] + by, radices[level])
        return to, me + (to - digits[level]) * strides[level]

    group = []
    for offsets in itertools.product(*[range(r) for r in radices[:local]]):
        if any(offsets):
            there, index = [], me
            for level, by in zip(range(local), offsets):
                to, _ = peer(level, by)
                there.append(to)
                index = index + (to - digits[level]) * strides[level]
            group.append((tuple(there), index))

    other = {"replica": lax.rem(rep + 1, replicas)}

    def columns(k):
        return slice(sum(widths[:k]), sum(widths[: k + 1]))

    loads = [
        pltpu.make_async_copy(attn_hbm, attn_raw, in_sem.at[0]),
        pltpu.make_async_copy(mom_hbm, mom, in_sem.at[1]),
        pltpu.make_async_copy(target_hbm.at[me], target, in_sem.at[2]),
    ]
    proj_loads = [
        pltpu.make_async_copy(proj_hbm.at[:, columns(k)], proj[k].at[own], proj_sem.at[k])
        for k in range(chunks)
    ]
    loads[0].start()
    for load in proj_loads:
        load.start()
    loads[1].start()
    loads[2].start()

    barrier = pltpu.get_barrier_semaphore()
    greet = [{"tensor": index} for _, index in group]
    for level in range(local, levels):
        greet += [{"tensor": peer(level, by)[1]} for by in range(1, radices[level])]
    if mixing:
        greet.append(other)
    for device in greet:
        pl.semaphore_signal(barrier, inc=1, device_id=device, device_id_type=MESH)
    loads[0].wait()
    for at in blocks:
        attn[at] = attn_raw[tuple(reversed(at))]
    pl.semaphore_wait(barrier, len(greet))

    copies = {}

    def send(key, src, dst, send_sem, recv_sem, device):
        copy = pltpu.make_async_remote_copy(
            src_ref=src,
            dst_ref=dst,
            send_sem=send_sem,
            recv_sem=recv_sem,
            device_id=device,
            device_id_type=MESH,
        )
        copy.start()
        copies[key] = copy

    for i, (there, index) in enumerate(group):
        send(
            ("a", i),
            attn.at[there],
            attn_group.at[own],
            a_send.at[i],
            a_recv.at[i],
            {"tensor": index},
        )

    def gather(kind, ref, sems, level, k):
        place = tuple(digits[: level + 1])
        for by in range(1, radices[level]):
            send(
                (kind, level, k, by),
                ref[k].at[place],
                ref[k].at[place],
                sems[0].at[level, k, by - 1],
                sems[1].at[level, k, by - 1],
                {"tensor": peer(level, by)[1]},
            )

    def share_proj(level, k):
        gather("p", proj, (p_send, p_recv), level, k)

    def share_grad(level, k):
        gather("g", grads, (ag_send, ag_recv), level, k)

    def reduce_start(level, k):
        for by in range(1, radices[level]):
            to, index = peer(level, by)
            send(
                ("r", level, k, by),
                sums[level - local][k].at[to],
                landed[level - local][k].at[by - 1],
                rs_send.at[level, k, by - 1],
                rs_recv.at[level, k, by - 1],
                {"tensor": index},
            )

    def wait_recv(kind, level, k):
        for by in range(1, radices[level]):
            copies[kind, level, k, by].wait_recv()

    def first(k):
        proj_loads[k].wait()
        if local > 0:
            share_proj(local - 1, k)

    def proj_stage(level, k):
        wait_recv("p", level, k)
        share_proj(level - 1, k)

    def product(k):
        if local > 0:
            wait_recv("p", 0, k)
        if k == 0:
            for i in range(len(group)):
                copies["a", i].wait_recv()
        part = jnp.zeros((tokens // len_group, widths[k]), F32)
        for at in itertools.product(*[range(r) for r in radices[:local]]):
            left = attn_group[at]
            part = part + jnp.dot(flat(left), proj[k][at], preferred_element_type=F32)
        shape = tuple(radices[local:]) + (rows, widths[k])
        part = part.reshape(shape)
        if outer > 0:
            sums[0][k][...] = part.astype(BF16)
            reduce_start(local, k)
        else:
            finish(part, k)

    def flat(block):
        count = 1
        for n in block.shape[:-1]:
            count *= n
        if rows % 16:
            return block.astype(F32).reshape(count, block.shape[-1]).astype(BF16)
        return block.reshape(count, block.shape[-1])

    def reduce_stage(level, k):
        wait_recv("r", level, k)
        value = sums[level - local][k][digits[level]].astype(F32)
        for by in range(1, radices[level]):
            value = value + landed[level - local][k][by - 1].astype(F32)
        if level + 1 < levels:
            sums[level + 1 - local][k][...] = value.astype(BF16)
            reduce_start(level + 1, k)
        else:
            finish(value, k)

    def finish(value, k):
        if k == 0:
            loads[2].wait()
        summed = value * scaling
        grad = (summed - target[:, columns(k)].astype(F32)) * weights
        grads[k][mine] = grad.astype(BF16)
        share_grad(levels - 1, k)
        projected_ref[:, columns(k)] = summed.astype(BF16)

    def gather_stage(level, k):
        wait_recv("g", level, k)
        if level > 0:
            share_grad(level - 1, k)
            return
        if k == 0:
            loads[1].wait()
        block = flat(grads[k][...])
        weight = proj[k][own]
        gradient = jnp.dot(attn_t[...], block, preferred_element_type=F32) * scaling
        moment = (BETA_MOM * mom[:, columns(k)].astype(F32) + gradient).astype(BF16)
        if mixing:
            moments[k][...] = moment
            send(
                ("y", k),
                moments[k],
                partner_moments[k],
                y_send.at[k],
                y_recv.at[k],
                other,
            )
        else:
            put(k, updated_of(weight, moment), moment)
        total[...] += lax.dot_general(
            block, weight, (((1,), (1,)), ((), ())), preferred_element_type=F32
        )

    def put(k, new_proj, new_moment):
        out_proj_ref[:, columns(k)] = new_proj
        out_mom_ref[:, columns(k)] = new_moment

    def updated_of(weight, moment):
        return (weight.astype(F32) - STEP_RATE * moment.astype(F32)).astype(BF16)

    def mix_stage(k):
        if not mixing:
            return
        if k == 0:
            copies["yp"].wait_recv()
        copies["y", k].wait_recv()
        ours, theirs = moments[k][...], partner_moments[k][...]
        one = updated_of(proj[k][own], ours).astype(F32)
        two = updated_of(partner_proj[:, columns(k)], theirs).astype(F32)
        put(
            k,
            ((one + two) * 0.5).astype(BF16),
            ((ours.astype(F32) + theirs.astype(F32)) * 0.5).astype(BF16),
        )

    len_group = len(group) + 1
    stages = [first]
    stages += [partial(proj_stage, level) for level in range(local - 1, 0, -1)]
    stages += [product]
    stages += [partial(reduce_stage, level) for level in range(local, levels)]
    stages += [partial(gather_stage, level) for level in range(levels - 1, -1, -1)]
    stages += [mix_stage]

    shares = tuple(width / widths[0] for width in widths)
    order = order_of(hops_of(radices, local, rows, depth, widths[0]), shares)
    ahead = 0
    while ahead < len(order) and order[ahead][0] == 0:
        first(order[ahead][1])
        ahead += 1
    if mixing:
        send("yp", proj_hbm, partner_proj, y_send.at[chunks], y_recv.at[chunks], other)
    attn_group[own] = attn[own]

    seg = seg_ref[...].astype(F32)
    shape = (rows, tokens)
    row_at = lax.broadcasted_iota(jnp.int32, shape, 0) + me * rows
    col_at = lax.broadcasted_iota(jnp.int32, shape, 1)
    seg_all = jnp.broadcast_to(seg, shape)
    own_seg = jnp.sum(jnp.where(row_at == col_at, seg_all, 0.0), axis=1, keepdims=True)
    count = jnp.sum(jnp.where(seg_all == own_seg, 1.0, 0.0), axis=1, keepdims=True)
    weights = tokens / (SEGS * count)
    attn_t[...] = flat(attn[...]).T
    total[...] = jnp.zeros_like(total)

    for j, k in order[ahead:]:
        stages[j](k)

    for i, at in enumerate(blocks):
        place = sum(digit * stride for digit, stride in zip(at, strides))
        attn_grad_ref[place] = (total[i * rows : (i + 1) * rows, :] * scaling).astype(BF16)
    for copy in copies.values():
        copy.wait_send()


def per_chunk(widths, shape):
    return [pltpu.VMEM(tuple(shape) + (width,), BF16) for width in widths]


def fused(attn, proj, mom, seg, target, radices, replicas, mixing):
    size, rows, wide = target.shape
    tokens, depth = size * rows, proj.shape[0]
    widths = tuple(wide // sum(SHARES) * share for share in SHARES)
    chunks = len(widths)
    levels = len(radices)
    local = min(2, levels)
    most = max(radices) - 1
    scaling = (depth * size) ** (-0.5)
    dims = tuple(radices)
    sums, landed = [], []
    for level in range(local, levels):
        high = dims[level + 1 :]
        sums.append(per_chunk(widths, (radices[level],) + high + (rows,)))
        landed.append(per_chunk(widths, (radices[level] - 1,) + high + (rows,)))
    local_dims, outer_dims = dims[:local], dims[local:]
    group = 1
    for radix in local_dims:
        group *= radix
    vmem = pl.BlockSpec(memory_space=pltpu.VMEM)
    any_place = pl.BlockSpec(memory_space=pl.ANY)
    dma = pltpu.SemaphoreType.DMA
    return pl.pallas_call(
        functools.partial(kernel, radices, local, replicas, widths, mixing, scaling),
        out_shape=(
            jax.ShapeDtypeStruct((rows, wide), BF16),
            jax.ShapeDtypeStruct((size, rows, depth), BF16),
            jax.ShapeDtypeStruct((depth, wide), BF16),
            jax.ShapeDtypeStruct((depth, wide), BF16),
        ),
        in_specs=[
            any_place,
            any_place,
            any_place,
            vmem,
            any_place,
        ],
        out_specs=(vmem,) * 4,
        scratch_shapes=[
            sums,
            landed,
            pltpu.VMEM(tuple(reversed(dims)) + (rows, depth), BF16),
            pltpu.VMEM(dims + (rows, depth), BF16),
            pltpu.VMEM(local_dims + outer_dims + (rows, depth), BF16),
            per_chunk(widths, local_dims + (depth,)),
            pltpu.VMEM((depth, wide), BF16),
            pltpu.VMEM((rows, wide), BF16),
            per_chunk(widths, dims + (rows,)),
            per_chunk(widths, (depth,)),
            per_chunk(widths, (depth,)),
            pltpu.VMEM((depth, wide), BF16),
            pltpu.VMEM((depth, tokens), BF16),
            pltpu.VMEM((tokens, depth), F32),
            dma((3,)),
            dma((chunks,)),
            dma((group,)),
            dma((group,)),
            dma((levels, chunks, most)),
            dma((levels, chunks, most)),
            dma((levels, chunks, most)),
            dma((levels, chunks, most)),
            dma((levels, chunks, most)),
            dma((levels, chunks, most)),
            dma((chunks + 1,)),
            dma((chunks + 1,)),
        ],
        cost_estimate=pl.CostEstimate(
            flops=6 * tokens * depth * wide, bytes_accessed=8 * depth * wide, transcendentals=0
        ),
        compiler_params=pltpu.CompilerParams(
            collective_id=0, has_side_effects=True, vmem_limit_bytes=VMEM_BYTES
        ),
    )(attn.reshape(tuple(reversed(dims)) + (rows, depth)), proj, mom, seg, target)


def passed_along(x, axis, by):
    size = lax.axis_size(axis)
    return lax.ppermute(x, axis, [(i, (i + by) % size) for i in range(size)])


def on_device(attn_out, proj, momentum, target, segment_ids, step):
    tensor_size = lax.axis_size("tensor")
    replicas = lax.axis_size("replica")
    rows_each = target.shape[1] // tensor_size
    bits = replicas.bit_length() - 1
    projected, attn_grad, updated, moment = fused(
        attn_out[0],
        proj[0],
        momentum[0],
        segment_ids,
        target[0].reshape(tensor_size, rows_each, target.shape[2]),
        radices_of(tensor_size),
        replicas,
        replicas == 2,
    )
    if replicas > 2:
        stacked = jnp.stack((updated, moment))
        branches = [
            partial(passed_along, axis="replica", by=1 << bit_pos) for bit_pos in range(bits)
        ]
        partner = lax.switch(step[0] % bits, branches, stacked)
        mixed = ((stacked.astype(F32) + partner.astype(F32)) * 0.5).astype(BF16)
        updated, moment = mixed[0], mixed[1]
    attn_grad = attn_grad.reshape(attn_out.shape)
    return (projected[None], attn_grad, updated[None], moment[None])


def solution(mesh):
    return jax.shard_map(
        on_device,
        mesh=mesh,
        in_specs=(
            P("replica", None, "tensor"),
            P("replica", "tensor", None),
            P("replica", "tensor", None),
            P("replica", None, None),
            P("replica", None),
            P(),
        ),
        out_specs=(
            P("replica", "tensor", None),
            P("replica", None, "tensor"),
            P("replica", "tensor", None),
            P("replica", "tensor", None),
        ),
        check_vma=False,
    )
```
